512 devices in a mesh: sect: 2 (over y_hi), exp: 32 (over z, y_lo), dp: 8 (over x, core).
Axes of the slice: x: 4, y: 4 (y_hi: 2, y_lo: 2; y = y_hi * 2 + y_lo), z: 16, core: 2. Of those that a mesh axis runs over, the one named last changes fastest.
Arguments:
- decode_states: bfloat16 [1024, 2048], P('exp'), may hold values from -15 to 15
- norm_gain: float32 [2048], replicated, may hold values from 0.25 to 1.75
- decode_routes: int32 [4, 1024, 2], P(None, 'exp'), may hold values from 0 to 31, all different within a row; in each aligned block of 32 rows (0 to 31, 32 to 63, ..., all dimensions but the last counted through in order) at most 3 rows name the same one
- decode_gates: float32 [4, 1024, 2], P(None, 'exp'), may hold values from 0.2 to 1
- up_weight: bfloat16 [2, 32, 1536, 2048], P('sect', 'exp', 'dp'), may hold values from -5 to 5
- down_weight: bfloat16 [2, 32, 1536, 2048], P('sect', 'exp', 'dp'), may hold values from -5 to 5
- traj_inputs: bfloat16 [2, 1024, 2048], P('sect', 'exp'), may hold values from -6 to 6
- traj_cotangents: bfloat16 [2, 1024, 2048], P('sect', 'exp'), may hold values from -6 to 6
- traj_lengths: int32 [32, 2, 16], P('exp'), may hold values from 1 to 4, 32 in all within a row
- packing: int32 [32, 32], P('exp'), may hold values from 0 to 31, each once within a row
- learner_routes: int32 [4096, 2], P('exp'), may hold values from 0 to 31, all different within a row; in each aligned block of 128 rows (0 to 127, 128 to 255, ...) at most 12 rows name the same one
- learner_gates: float32 [4096, 2], P('exp'), may hold values from 0.2 to 1
Outputs:
- final_states: bfloat16 [1024, 2048], P('exp', 'sect')
- fresh_up: bfloat16 [2, 32, 1536, 2048], P('sect', 'exp', 'dp')
- fresh_down: bfloat16 [2, 32, 1536, 2048], P('sect', 'exp', 'dp')
The draws below stay inside these ranges and needn't reach their ends.
Inputs may be any that keep to these rules, and one draw needn't show every extreme that they name: `decode_routes`: within each aligned block of 32 rows of one step (the rows of one index of exp), no expert is named more than 3 times, and that bound is met. `learner_routes`: within each aligned block of 128 rows (the slots of one learner shard), no expert is named more than 12 times, and that bound is met. `traj_lengths`: each row of 16 lengths sums to 32 and its largest is 4. `packing`: each row is a permutation of the 32 learner shards, so every holder sends exactly one trajectory to every shard.
All inputs are finite; a program needn't handle non-finite values.
Results may differ from the reference program's by a relative error of at most 0.02.
Values may be sent and summed in bfloat16 or wider, within the bound.
A program may use at most 64 MiB of HBM per device.

```python
import math
import jax
import jax.numpy as jnp
import numpy as np
from jax import lax

D = 2048
H = 1536
K = 2
STEPS = 4
DEC_ROWS = 32
LRN_ROWS = 128
EXPERTS = 32
ROWS = 1024
CAP_D = 3
CAP_L = 12
CAP_T = 4
NT = 16
SRC_ROWS = 32
N_EXP = 32
N_DP = 8


def draw_decode_states(key, part):
    key_values = jax.random.fold_in(key, 11)
    key_rows = jax.random.fold_in(key, 12)
    key_cols = jax.random.fold_in(key, 13)
    row_scale = jnp.exp(jax.random.uniform(key_rows, (ROWS, 1), jnp.float32, 0.0, 2.302585))
    col_scale = jnp.exp(jax.random.uniform(key_cols, (1, D), jnp.float32, 0.0, 2.302585))
    unit_values = jnp.clip(jax.random.normal(key_values, (ROWS, D), jnp.float32), -5.0, 5.0)
    return (0.03 * unit_values * row_scale * col_scale).astype(jnp.bfloat16)


def steps_of(own_key, shape, cuts, least, high):
    factor_of = 1.0
    for position, blocks in cuts:
        heights = jax.random.uniform(jax.random.fold_in(jax.random.fold_in(own_key, 6), position), (blocks,), jnp.float32, least / len(cuts), high / len(cuts))
        factor_of = factor_of * jnp.repeat(jnp.exp(heights), shape[position] // blocks).reshape((-1,) + (1,) * (len(shape) - 1 - position))
    return factor_of


def length_profile(amount, total, reach, slope):
    weights = [(1 << 20) // math.isqrt(standing ** slope) + 1 for standing in range(2, amount + 1)]
    rest, counts = total - reach - (amount - 1), [1] * (amount - 1)
    while rest > 0:
        candidates = [i for i in range(amount - 1) if counts[i] < reach]
        mass, remaining = sum([weights[i] for i in candidates]), rest
        for i in candidates:
            more = min(reach - counts[i], max(1, remaining * weights[i] // mass), rest)
            counts[i] = counts[i] + more
            rest = rest - more
    return np.array([reach] + counts)


def ragged(stream_key, number_of, total, reach, slope):
    if number_of == 2:
        one = jax.random.randint(stream_key, (), max(1, total - reach), min(reach, total - 1) + 1)
        return jnp.stack([one, total - one])
    tallies = jnp.asarray(length_profile(number_of, total, reach, slope), jnp.int32)
    couples = (number_of - 1) // 2
    source_of, taker = tallies[1:1 + 2 * couples:2], tallies[2:2 + 2 * couples:2]
    slack = jnp.minimum(source_of - 1, reach - taker)
    shifted = jax.random.randint(jax.random.fold_in(stream_key, 1), (couples,), 0, 1 << 20) % (slack + 1)
    tallies = tallies.at[1:1 + 2 * couples:2].set(source_of - shifted).at[2:2 + 2 * couples:2].set(taker + shifted)
    return tallies[jax.random.permutation(jax.random.fold_in(stream_key, 2), number_of)]


def shared_out(key, own, number, rows, amount, top, most, skew):
    ranking = jax.random.permutation(key, amount)
    packed, ordinary = portions_of(amount, rows * top, most, skew, True), portions_of(amount, rows * top, most, skew, False)
    places = jnp.arange(amount)

    def named(sizes, offset_by):
        used = int((sizes > 0).sum())
        fixed = max(1, used // 4)
        moved = fixed + (places - fixed + offset_by * (used - fixed)) % max(1, amount - fixed)
        return jnp.zeros((amount,), jnp.int32).at[ranking[jnp.where(places < fixed, places, moved)]].set(jnp.asarray(sizes, jnp.int32))

    sizes = jnp.where(number % 4 == 0, named(packed, number // 4), named(ordinary, number - number // 4 - 1))
    mixed = jax.random.permutation(jax.random.fold_in(own, 3), amount)
    giver, taker = mixed[0:amount // 2 * 2:2], mixed[1:amount // 2 * 2:2]
    room = jnp.minimum(sizes[giver] - 1, most - sizes[taker]) // 2
    room = jnp.where((giver == ranking[0]) | (taker == ranking[0]) | (sizes[taker] == 0), 0, jnp.maximum(room, 0))
    moved = jax.random.randint(jax.random.fold_in(own, 4), (amount // 2,), 0, 1 << 20) % (room + 1)
    sizes = sizes.at[giver].add(-moved).at[taker].add(moved)
    items = jnp.searchsorted(jnp.cumsum(sizes), jnp.arange(rows * top), side="right").astype(jnp.int32)
    grid = items.reshape(top, rows).T
    grid = grid[jax.random.permutation(jax.random.fold_in(own, 1), rows)]
    offset_by = jax.random.randint(jax.random.fold_in(own, 2), (rows, 1), 0, top)
    return jnp.take_along_axis(grid, (jnp.arange(top)[None, :] + offset_by) % top, axis=1)


def portions_of(amount, total, bound, skew, full):
    weights = [(1 << 20) // math.isqrt(grade ** skew) + 1 for grade in range(1, amount + 1)]
    largest = bound if full else min(bound, max(-(-total // amount), total * weights[0] // sum(weights)))
    least = 1 if total - largest >= amount - 1 else 0
    given, rest = [largest] + [least] * (amount - 1), total - largest - least * (amount - 1)
    while rest > 0:
        candidates = [i for i in range(1, amount) if given[i] < largest] or [i for i in range(1, amount) if given[i] < bound]
        mass, remaining = sum([weights[i] for i in candidates]), rest
        for i in candidates:
            addition = min(bound - given[i], max(1, remaining * weights[i] // mass), rest)
            given[i] = given[i] + addition
            rest = rest - addition
    return np.array(given)


def normal_values(rng, shape, spread, bound, shards=(), held_as=jnp.bfloat16):
    result = spread * jax.random.normal(rng, shape, jnp.float32)
    if shards:
        result = result * steps_of(rng, shape, shards, -0.22, 0.18)
    return jnp.clip(result, -bound, bound).astype(held_as)


def setup_inputs(seed: int = 0) -> dict:
    streams_of = jax.random.split(jax.random.key(seed), 13)
    decode_states = draw_decode_states(jax.random.fold_in(streams_of[12], 71), 0)
    norm_gain = jnp.clip(1.0 + 0.15 * jax.random.normal(streams_of[1], (D,), jnp.float32), 0.25, 1.75)
    decode_routes_keys = jax.random.split(jax.random.fold_in(streams_of[2], 1), STEPS * ROWS // DEC_ROWS)
    decode_routes_turns = jax.random.permutation(jax.random.fold_in(streams_of[2], 3), STEPS * ROWS // DEC_ROWS)
    decode_routes = jax.vmap(lambda own, number: shared_out(jax.random.fold_in(streams_of[2], 2), own, number, DEC_ROWS, N_EXP, K, CAP_D, 2))(decode_routes_keys, decode_routes_turns).reshape((STEPS, ROWS, K))
    decode_gates = jnp.clip(0.2 + 0.8 * jax.random.uniform(streams_of[3], (STEPS, ROWS, K), jnp.float32) ** steps_of(streams_of[3], (STEPS, ROWS, K), ((1, 32),), -0.2, 0.2), 0.2, 1.0)
    up_weight = normal_values(streams_of[4], (2, EXPERTS, H, D), 1.0, 5.0, ((0, 2), (1, 32), (2, 8)))
    down_weight = normal_values(streams_of[5], (2, EXPERTS, H, D), 1.0, 5.0, ((0, 2), (1, 32), (2, 8)))
    traj_inputs = normal_values(streams_of[6], (2, N_EXP * SRC_ROWS, D), 1.0, 6.0, ((0, 2), (1, 32)))
    traj_cotangents = normal_values(streams_of[7], (2, N_EXP * SRC_ROWS, D), 1.0, 6.0, ((0, 2), (1, 32)))
    traj_lengths = jax.vmap(lambda own: ragged(own, NT, SRC_ROWS, CAP_T, 2))(jax.random.split(streams_of[8], N_EXP * 2)).reshape((N_EXP, 2, NT)).astype(jnp.int32)
    packing = jax.vmap(lambda own: jax.random.permutation(own, N_EXP))(jax.random.split(streams_of[9], N_EXP)).reshape((N_EXP, N_EXP)).astype(jnp.int32)
    learner_routes_keys = jax.random.split(jax.random.fold_in(streams_of[10], 1), (N_EXP * LRN_ROWS) // LRN_ROWS)
    learner_routes_turns = jax.random.permutation(jax.random.fold_in(streams_of[10], 3), (N_EXP * LRN_ROWS) // LRN_ROWS)
    learner_routes = jax.vmap(lambda own, number: shared_out(jax.random.fold_in(streams_of[10], 2), own, number, LRN_ROWS, N_EXP, K, CAP_L, 2))(learner_routes_keys, learner_routes_turns).reshape((N_EXP * LRN_ROWS, K))
    learner_gates = jnp.clip(0.2 + 0.8 * jax.random.uniform(streams_of[11], (N_EXP * LRN_ROWS, K), jnp.float32) ** steps_of(streams_of[11], (N_EXP * LRN_ROWS, K), ((0, 32),), -0.2, 0.2), 0.2, 1.0)
    return dict(decode_states=decode_states, norm_gain=norm_gain, decode_routes=decode_routes, decode_gates=decode_gates, up_weight=up_weight, down_weight=down_weight, traj_inputs=traj_inputs, traj_cotangents=traj_cotangents, traj_lengths=traj_lengths, packing=packing, learner_routes=learner_routes, learner_gates=learner_gates)


step_size = 3.0
norm_eps = 1e-06
highest = lax.Precision.HIGHEST

def slot_table(routes, capacity):
    flat_routes = routes.reshape(-1).astype(jnp.int32)
    member = (flat_routes[:, None] == jnp.arange(EXPERTS, dtype=jnp.int32)[None, :]).astype(jnp.int32)
    earlier = (jnp.cumsum(member, axis=0) - member).astype(jnp.int32)
    within = lax.optimization_barrier(jnp.sum(earlier * member, axis=1)).astype(jnp.int32)
    target = flat_routes * capacity + within
    one_hot = (target[:, None] == jnp.arange(EXPERTS * capacity, dtype=jnp.int32)[None, :]).astype(jnp.float32)
    return one_hot.reshape(routes.shape[0], routes.shape[1], EXPERTS * capacity)

def pack_rows(held_rows, lengths, row_pack):
    traj_count = lengths.shape[1]
    per_half = held_rows.shape[0] // 2
    column_ids = jnp.arange(row_pack.shape[0], dtype=jnp.int32)
    starts = (jnp.cumsum(lengths, axis=1) - lengths).astype(jnp.int32)
    matches = (row_pack[None, :] == column_ids[:, None]).astype(jnp.int32)
    chosen = lax.optimization_barrier(jnp.sum(matches * column_ids[None, :], axis=1)).astype(jnp.int32)
    half_index = chosen // traj_count
    length_of = jnp.take(lengths.reshape(-1), chosen)
    first_row = half_index * per_half + jnp.take(starts.reshape(-1), chosen)
    offsets = jnp.arange(CAP_T, dtype=jnp.int32)
    in_length = offsets[None, :] < length_of[:, None]
    row_index = jnp.where(in_length, first_row[:, None] + offsets[None, :], 0).reshape(-1).astype(jnp.int32)
    picked = jnp.take(held_rows, row_index, axis=0)
    return jnp.where(in_length.reshape(-1)[:, None, None], picked, jnp.zeros_like(picked))

def update_expert(operands):
    inputs, scaled_grad, up_mat, down_mat = operands
    before_act = jnp.einsum('sd,hd->sh', inputs.astype(jnp.float32), up_mat.astype(jnp.float32), precision=highest) * D ** (-0.5)
    sigmoid_val = jax.nn.sigmoid(before_act)
    activated = (before_act * sigmoid_val).astype(jnp.bfloat16)
    hidden_grad = jnp.einsum('sd,hd->sh', scaled_grad.astype(jnp.float32), down_mat.astype(jnp.float32), precision=highest) * H ** (-0.5)
    pre_grad = (hidden_grad * sigmoid_val * (1.0 + before_act * (1.0 - sigmoid_val))).astype(jnp.bfloat16)
    down_grad = jnp.einsum('sh,sd->hd', activated.astype(jnp.float32), scaled_grad.astype(jnp.float32), precision=highest) * H ** (-0.5)
    up_grad = jnp.einsum('sh,sd->hd', pre_grad.astype(jnp.float32), inputs.astype(jnp.float32), precision=highest) * D ** (-0.5)
    new_up = (up_mat.astype(jnp.float32) - step_size * up_grad).astype(jnp.bfloat16)
    new_down = (down_mat.astype(jnp.float32) - step_size * down_grad).astype(jnp.bfloat16)
    return (new_up, new_down)

def learner_fresh(up_weight, down_weight, traj_inputs, traj_cotangents, traj_lengths, packing, learner_routes, learner_gates):
    pairs = jnp.stack([traj_inputs, traj_cotangents], axis=2)
    holders = pairs.reshape(2, N_EXP, SRC_ROWS, 2, D).transpose(1, 0, 2, 3, 4).reshape(N_EXP, 2 * SRC_ROWS, 2, D)
    outgoing = lax.map(lambda operands: pack_rows(operands[0], operands[1], operands[2]), (holders, traj_lengths, packing))
    batches = outgoing.reshape(N_EXP, EXPERTS, CAP_T, 2, D).transpose(1, 0, 2, 3, 4).reshape(EXPERTS, LRN_ROWS, 2, D)
    shard_routes = learner_routes.reshape(N_EXP, LRN_ROWS, K)
    shard_gates = learner_gates.reshape(N_EXP, LRN_ROWS, K)
    one_hots = jax.vmap(lambda route_block: slot_table(route_block, CAP_L))(shard_routes)
    token_part = jnp.einsum('erks,erd->esd', one_hots, batches[:, :, 0, :].astype(jnp.float32), precision=highest).astype(jnp.bfloat16)
    grad_part = jnp.einsum('erks,erd->esd', one_hots * shard_gates[:, :, :, None], batches[:, :, 1, :].astype(jnp.float32), precision=highest).astype(jnp.bfloat16)
    token_in = token_part.reshape(N_EXP, EXPERTS, CAP_L, D).transpose(1, 0, 2, 3).reshape(EXPERTS, N_EXP * CAP_L, D)
    grad_in = grad_part.reshape(N_EXP, EXPERTS, CAP_L, D).transpose(1, 0, 2, 3).reshape(EXPERTS, N_EXP * CAP_L, D)
    return lax.map(update_expert, (token_in, grad_in, up_weight[1], down_weight[1]))

def expert_forward(operands):
    slot_rows, up_mat, down_mat = operands
    before_act = jnp.einsum('sd,hd->sh', slot_rows.astype(jnp.float32), up_mat.astype(jnp.float32), precision=highest) * D ** (-0.5)
    activated = jax.nn.silu(before_act).astype(jnp.bfloat16)
    act_blocks = activated.reshape(slot_rows.shape[0], N_DP, H // N_DP).astype(jnp.float32)
    down_blocks = down_mat.reshape(N_DP, H // N_DP, D).astype(jnp.float32)
    parts = (jnp.einsum('snh,nhd->nsd', act_blocks, down_blocks, precision=highest) * H ** (-0.5)).astype(jnp.bfloat16)
    return lax.optimization_barrier(jnp.sum(parts.astype(jnp.float32), axis=0)).astype(jnp.bfloat16)

def decode_step(states, norm_gain, routes, gate_values, up_all, down_all):
    normed = (states * lax.rsqrt(lax.optimization_barrier(jnp.mean(states * states, axis=1, keepdims=True)) + norm_eps) * norm_gain).astype(jnp.bfloat16)
    src_routes = routes.reshape(N_EXP, DEC_ROWS, K)
    one_hots = jax.vmap(lambda route_block: slot_table(route_block, CAP_D))(src_routes)
    outgoing = jnp.einsum('erks,erd->esd', one_hots, normed.reshape(N_EXP, DEC_ROWS, D).astype(jnp.float32), precision=highest).astype(jnp.bfloat16)
    arrived = outgoing.reshape(N_EXP, EXPERTS, CAP_D, D).transpose(1, 0, 2, 3).reshape(EXPERTS, N_EXP * CAP_D, D)
    results = lax.map(expert_forward, (arrived, up_all, down_all))
    returned = results.reshape(EXPERTS, N_EXP, CAP_D, D).transpose(1, 0, 2, 3).reshape(N_EXP, EXPERTS * CAP_D, D)
    weighted = one_hots * gate_values.reshape(N_EXP, DEC_ROWS, K)[:, :, :, None]
    mixed = jnp.einsum('erks,esd->erd', weighted, returned.astype(jnp.float32), precision=highest)
    return states + mixed.reshape(ROWS, D)

def reference(decode_states, norm_gain, decode_routes, decode_gates, up_weight, down_weight, traj_inputs, traj_cotangents, traj_lengths, packing, learner_routes, learner_gates):
    fresh_up, fresh_down = learner_fresh(up_weight, down_weight, traj_inputs, traj_cotangents, traj_lengths, packing, learner_routes, learner_gates)
    states = decode_states.astype(jnp.float32)
    for step_index in range(STEPS):
        if step_index < STEPS // 2:
            up_all = up_weight[0]
            down_all = down_weight[0]
        else:
            up_all = fresh_up
            down_all = fresh_down
        states = decode_step(states, norm_gain, decode_routes[step_index], decode_gates[step_index], up_all, down_all)
    return (states.astype(jnp.bfloat16), jnp.stack([fresh_up, fresh_up]), jnp.stack([fresh_down, fresh_down]))
```

```python
import functools

import jax
import jax.numpy as jnp
import ml_dtypes
import numpy as np
from jax import lax
from jax.experimental import pallas as pl
from jax.experimental.pallas import tpu as pltpu
from jax.sharding import PartitionSpec as P

MESH = pl.DeviceIdType.MESH
step_size = 3.0
norm_eps = 1e-06
f32 = jnp.float32
bf16 = jnp.bfloat16
LANES = 128
GROUPS = 4


def dot(a, b):
    return lax.dot_general(a, b, (((1,), (0,)), ((), ())), preferred_element_type=f32)


def dot_nt(a, b):
    return lax.dot_general(a, b, (((1,), (1,)), ((), ())), preferred_element_type=f32)


def dot_tn(a, b):
    return lax.dot_general(a, b, (((0,), (0,)), ((), ())), preferred_element_type=f32)


def iota(shape, dim):
    return lax.broadcasted_iota(jnp.int32, shape, dim).astype(f32)


def to_row(col):
    n = col.shape[0]
    eye = iota((n, n), 0) == iota((n, n), 1)
    return jnp.sum(jnp.where(eye, col, 0.0), axis=0, keepdims=True)


def to_col(row):
    n = row.shape[1]
    eye = iota((n, n), 0) == iota((n, n), 1)
    return jnp.sum(jnp.where(eye, row, 0.0), axis=1, keepdims=True)


def ranks(first, second):
    n = first.shape[0]
    first_row, second_row = to_row(first), to_row(second)
    before = iota((n, n), 1) < iota((n, n), 0)
    out = []
    for mine in (first, second):
        same = ((first_row == mine) | (second_row == mine)) & before
        out.append(jnp.sum(jnp.where(same, 1.0, 0.0), axis=1, keepdims=True))
    return out


def permutations(experts, cap_d, cap_l):
    slots = experts * cap_d
    take_d = np.zeros((2 * slots, experts * 8), np.float32)
    for c in range(2):
        for k in range(experts):
            for s in range(cap_d):
                take_d[c * slots + k * cap_d + s, k * 8 + c * 4 + s] = 1
    give_d = np.stack([take_d[:slots].T, take_d[slots:].T])
    per = experts // GROUPS
    take_l = np.zeros((per * cap_l * 2, per * cap_l * 2), np.float32)
    for c in range(2):
        for k in range(per):
            for s in range(cap_l):
                take_l[c * per * cap_l + k * cap_l + s, k * 2 * cap_l + c * cap_l + s] = 1
    return [m.astype(ml_dtypes.bfloat16) for m in (take_d, give_d, take_l)]


def kernel(
    experts, shards, cap_d, cap_l,
    rows_ref, gain_ref, routes_ref, gates_ref, up_ref, down_ref, in_ref, cot_ref, len_ref, pack_ref,
    lroutes_ref, lgates_ref, take_d_ref, give_d_ref, take_l_ref,
    final_ref, fresh_up_ref, fresh_down_ref,
    d1_out, d1_in, xg, d3_out, d3_in, d4_out, d4_in, states_ref, trow_ref, tcol_ref,
    held, out2, recv2, out3, recv3, xg4, act_ref, pre_ref, fin_src,
    dec_sem, l1_sem, l2_sem, st_sem, fin_sem, fresh_sem, l3_send, l3_recv, l4_send, l4_recv,
):
    sect, me, dp = lax.axis_index("sect"), lax.axis_index("exp"), lax.axis_index("dp")
    ring, core = lax.div(dp, 2), lax.rem(dp, 2)
    other = 1 - sect
    width = rows_ref.shape[1]
    part = width // shards
    hidden = up_ref.shape[0]
    model_scale = width ** (-0.5)
    hidden_scale = (hidden * shards) ** (-0.5)
    dec_rows = rows_ref.shape[0]
    slots = experts * cap_d
    per = experts // GROUPS
    group_slots = per * cap_l
    col0 = pl.multiple_of(dp * part, part)

    def rcopy(src, dst, send, recv, device):
        return pltpu.make_async_remote_copy(
            src_ref=src, dst_ref=dst, send_sem=send, recv_sem=recv, device_id=device, device_id_type=MESH
        )

    def wait_sent(ref, sem):
        rcopy(ref, ref, sem, sem, (sect, me, dp)).wait_send()

    def wait_here(ref, sem):
        rcopy(ref, ref, sem, sem, (sect, me, dp)).wait_recv()

    def others(fn):
        def one(i, carry):
            half = lax.div(i + 1, 2)
            fn(jnp.where(lax.rem(i, 2) == 1, half, experts - half))
            return carry

        lax.fori_loop(1, experts, one, 0)

    barrier = pltpu.get_barrier_semaphore()

    def greet_exp(k):
        pl.semaphore_signal(barrier, inc=1, device_id=(sect, lax.rem(me + k, experts), dp), device_id_type=MESH)

    others(greet_exp)
    for q in range(1, shards):
        pl.semaphore_signal(barrier, inc=1, device_id=(sect, me, lax.rem(dp + q, shards)), device_id_type=MESH)
    for q in range(shards):
        pl.semaphore_signal(barrier, inc=1, device_id=(other, me, lax.rem(dp + q, shards)), device_id_type=MESH)
    pl.semaphore_wait(barrier, experts - 1 + shards - 1 + shards)

    @pl.when(sect == 0)
    def _():
        rcopy(in_ref.at[:, pl.ds(col0, part)], held.at[0], l1_sem.at[0], l1_sem.at[1], (other, me, dp)).start()
        rcopy(cot_ref.at[:, pl.ds(col0, part)], held.at[1], l1_sem.at[0], l1_sem.at[1], (other, me, dp)).start()

    def tables(i, t):
        routes = routes_ref[t].astype(f32)
        first, second = routes[:, 0:1], routes[:, 1:2]
        within = ranks(first, second)
        for k, mine in enumerate((first, second)):
            target = mine * 8.0 + within[k]
            both = jnp.concatenate([target, target + 4.0], axis=0)
            tcol_ref[i, k] = both
            trow_ref[i, k] = to_row(both)

    def decode_step(i, t, up, down):
        gain0, gain1 = gain_ref[pl.ds(2 * dp, 1), :], gain_ref[pl.ds(2 * dp + 1, 1), :]
        gains = jnp.concatenate(
            [jnp.broadcast_to(gain0, (dec_rows, LANES)), jnp.broadcast_to(gain1, (dec_rows, LANES))], axis=0
        )
        y = (states_ref[...] * gains).astype(bf16)
        row_ids = iota((experts * 8, 2 * dec_rows), 0)
        pick = (row_ids == trow_ref[i, 0]) | (row_ids == trow_ref[i, 1])
        pick = jnp.where(pick, 1.0, 0.0).astype(bf16)
        d1_out[i] = dot(pick, y).astype(bf16).reshape(experts, 8, LANES)
        d1_in[i, me] = d1_out[i, me]

        def send1(k):
            to = lax.rem(me + k, experts)
            rcopy(d1_out.at[i, to], d1_in.at[i, me], dec_sem.at[0, i, 0], dec_sem.at[0, i, 1], (sect, to, dp)).start()

        others(send1)
        wait_here(d1_in.at[i, pl.ds(0, experts - 1)], dec_sem.at[0, i, 1])
        block = dot(take_d_ref[...], d1_in[i].reshape(experts * 8, LANES)).astype(bf16)
        xg[i, dp] = jnp.concatenate([block[:slots], block[slots:]], axis=1)

        def send2(q, carry):
            to = lax.rem(dp + q, shards)
            rcopy(xg.at[i, dp], xg.at[i, dp], dec_sem.at[1, i, 0], dec_sem.at[1, i, 1], (sect, me, to)).start()
            return carry

        lax.fori_loop(1, shards, send2, 0)
        wait_here(xg.at[i, pl.ds(0, shards - 1)], dec_sem.at[1, i, 1])
        before_act = jnp.zeros((slots, hidden), f32)
        squares = jnp.zeros((slots, part), f32)
        for q in range(shards):
            piece = xg[i, q]
            before_act += dot_nt(piece, up[:, q * part : (q + 1) * part])
            gain = jnp.concatenate([gain_ref[2 * q : 2 * q + 1], gain_ref[2 * q + 1 : 2 * q + 2]], axis=1)
            wide = piece.astype(f32) / gain
            squares += wide * wide
        mean = jnp.sum(squares, axis=1, keepdims=True) * (1.0 / width)
        before_act = before_act * (lax.rsqrt(mean + norm_eps) * model_scale)
        act = (before_act / (1.0 + jnp.exp(-before_act))).astype(bf16)
        for q in range(shards):
            d3_out[i, q] = (dot(act, down[:, q * part : (q + 1) * part]) * hidden_scale).astype(bf16)
        d3_in[i, dp] = d3_out[i, dp]

        def send3(q, carry):
            to = lax.rem(dp + q, shards)
            rcopy(d3_out.at[i, to], d3_in.at[i, dp], dec_sem.at[2, i, 0], dec_sem.at[2, i, 1], (sect, me, to)).start()
            return carry

        lax.fori_loop(1, shards, send3, 0)
        wait_here(d3_in.at[i, pl.ds(0, shards - 1)], dec_sem.at[2, i, 1])
        total = d3_in[i, 0].astype(f32)
        for q in range(1, shards):
            total += d3_in[i, q].astype(f32)
        total = total.astype(bf16)
        back = dot(give_d_ref[0], total[:, :LANES]) + dot(give_d_ref[1], total[:, LANES:])
        d4_out[i] = back.astype(bf16).reshape(experts, 8, LANES)
        d4_in[i, me] = d4_out[i, me]

        def send4(k):
            to = lax.rem(me + k, experts)
            rcopy(d4_out.at[i, to], d4_in.at[i, me], dec_sem.at[3, i, 0], dec_sem.at[3, i, 1], (sect, to, dp)).start()

        others(send4)
        lane_ids = iota((2 * dec_rows, experts * 8), 1)
        gate = gates_ref[t]
        gate = jnp.concatenate([gate, gate], axis=0)
        mix = jnp.where(lane_ids == tcol_ref[i, 0], gate[:, 0:1], 0.0)
        mix += jnp.where(lane_ids == tcol_ref[i, 1], gate[:, 1:2], 0.0)
        high = mix.astype(bf16)
        rest = mix - high.astype(f32)
        middle = rest.astype(bf16)
        low = (rest - middle.astype(f32)).astype(bf16)
        wait_here(d4_in.at[i, pl.ds(0, experts - 1)], dec_sem.at[3, i, 1])
        returned = d4_in[i].reshape(experts * 8, LANES)
        states_ref[...] += dot(high, returned) + (dot(middle, returned) + dot(low, returned))

    def decode_sent(i):
        wait_sent(d1_out.at[i, pl.ds(0, experts - 1)], dec_sem.at[0, i, 0])
        wait_sent(xg.at[i, pl.ds(0, shards - 1)], dec_sem.at[1, i, 0])
        wait_sent(d3_out.at[i, pl.ds(0, shards - 1)], dec_sem.at[2, i, 0])
        wait_sent(d4_out.at[i, pl.ds(0, experts - 1)], dec_sem.at[3, i, 0])

    @pl.when(sect == 0)
    def _():
        for i in range(2):
            tables(i, i)
        states_ref[...] = jnp.concatenate(
            [
                rows_ref[:, pl.ds(col0, LANES)].astype(f32),
                rows_ref[:, pl.ds(pl.multiple_of(col0 + LANES, LANES), LANES)].astype(f32),
            ],
            axis=0,
        )
        for i in range(2):
            decode_step(i, i, up_ref, down_ref)
        move = rcopy(states_ref, states_ref, st_sem.at[0], st_sem.at[1], (other, me, dp))
        move.start()
        move.wait_send()
        wait_sent(held, l1_sem.at[0])
        for i in range(2):
            decode_sent(i)
        wait_here(fresh_up_ref, fresh_sem.at[0, 1])
        wait_here(fresh_down_ref, fresh_sem.at[1, 1])
        wait_here(final_ref, fin_sem.at[1])

    @pl.when(sect == 1)
    def _():
        lengths = len_ref[...].astype(f32)
        count = lengths.shape[1]
        length = jnp.concatenate([to_col(lengths[0:1]), to_col(lengths[1:2])], axis=0)
        both = 2 * count
        a, b = iota((both, both), 0), iota((both, both), 1)
        same_half = (a < count) == (b < count)
        start_row = jnp.sum(jnp.where(same_half & (a < b), length, 0.0), axis=0, keepdims=True)
        length_row = to_row(length)
        half_rows = held.shape[1]
        r, t = iota((2 * half_rows, both), 0), iota((2 * half_rows, both), 1)
        second = r >= half_rows
        row_in = r - jnp.where(second, float(half_rows), 0.0)
        offset = row_in - start_row
        inside = (second == (t >= count)) & (offset >= 0.0) & (offset < length_row)
        shard = pack_ref[...].astype(f32)
        target2 = jnp.sum(jnp.where(inside, shard * 8.0 + offset, 0.0), axis=1, keepdims=True)
        target2 = to_row(jnp.concatenate([target2, target2 + 4.0], axis=0))
        row_ids = iota((experts * 8, 4 * half_rows), 0)
        pack = jnp.where(row_ids == target2, 1.0, 0.0).astype(bf16)
        wait_here(held, l1_sem.at[1])
        for j, own_ref in enumerate((in_ref, cot_ref)):
            far = held[j]
            own = own_ref[:, pl.ds(col0, part)]
            stacked = jnp.concatenate([far[:, :LANES], own[:, :LANES], far[:, LANES:], own[:, LANES:]], axis=0)
            out2[j] = dot(pack, stacked).astype(bf16).reshape(experts, 8, LANES)
            recv2[j, me] = out2[j, me]

        def send_l2(k):
            to = lax.rem(me + k, experts)
            rcopy(out2.at[:, to], recv2.at[:, me], l2_sem.at[0], l2_sem.at[1], (sect, to, dp)).start()

        others(send_l2)

        lroutes = lroutes_ref[...].astype(f32)
        first, second = lroutes[:, 0:1], lroutes[:, 1:2]
        within = ranks(first, second)
        lgates = lgates_ref[...]

        def by_half(col, step):
            n = col.shape[0]
            row = jnp.zeros((1, 2 * n), f32)
            r, l = iota((n, 2 * n), 0), iota((n, 2 * n), 1)
            source = jnp.floor(r * 0.25)
            place = source * 4.0 + r
            row += jnp.sum(jnp.where(l == place, col, 0.0), axis=0, keepdims=True)
            row += jnp.sum(jnp.where(l == place + 4.0, col + step, 0.0), axis=0, keepdims=True)
            return row

        stride = 2.0 * cap_l
        tr0 = by_half(first * stride + within[0], float(cap_l))
        tr1 = by_half(second * stride + within[1], float(cap_l))
        gr0, gr1 = by_half(lgates[:, 0:1], 0.0), by_half(lgates[:, 1:2], 0.0)
        ids = iota((experts * 2 * cap_l, experts * 8), 0)
        hit0, hit1 = ids == tr0, ids == tr1
        pick = jnp.where(hit0 | hit1, 1.0, 0.0).astype(bf16)
        scale = jnp.where(hit0, gr0, 0.0) + jnp.where(hit1, gr1, 0.0)
        high = scale.astype(bf16)
        low = (scale - high.astype(f32)).astype(bf16)
        wait_here(recv2.at[:, pl.ds(0, experts - 1)], l2_sem.at[1])
        inputs = recv2[0].reshape(experts * 8, LANES)
        cots = recv2[1].reshape(experts * 8, LANES)
        out3[0] = dot(pick, inputs).astype(bf16).reshape(experts, 2 * cap_l, LANES)
        out3[1] = (dot(high, cots) + dot(low, cots)).astype(bf16).reshape(experts, 2 * cap_l, LANES)
        for g in range(GROUPS):

            def send_l3(n, carry, g=g):
                j = lax.rem(n, 2) * (per // 2) + lax.div(n, 2) if per > 1 else n
                to = lax.rem(me + j * GROUPS + g, experts)
                rcopy(out3.at[:, to], recv3.at[:, g * per + j], l3_send, l3_recv.at[g], (sect, to, dp)).start()
                return carry

            lax.fori_loop(1 if g == 0 else 0, per, send_l3, 0)
        recv3[0, 0] = out3[0, me]
        recv3[1, 0] = out3[1, me]

        nx = shards // 2
        right, left = lax.rem(ring + 1, nx), lax.rem(ring + nx - 1, nx)

        def at_ring(position):
            return (sect, me, position * 2 + core)

        def gather(g):
            first_in = 1 if g == 0 else 0
            if per - first_in:
                wait_here(recv3.at[:, pl.ds(g * per + first_in, per - first_in)], l3_recv.at[g])
            for j in range(2):
                rows = recv3[j, g * per : (g + 1) * per].reshape(per * 2 * cap_l, LANES)
                block = dot(take_l_ref[...], rows).astype(bf16)
                xg4[g, core, ring, j] = jnp.concatenate([block[:group_slots], block[group_slots:]], axis=1)
            mine = xg4.at[g, core, ring]
            rcopy(mine, mine, l4_send.at[0, g], l4_recv.at[0, g], at_ring(right)).start()
            rcopy(mine, mine, l4_send.at[1, g], l4_recv.at[1, g], at_ring(left)).start()

        def relay(g):
            from_left, from_right = xg4.at[g, core, left], xg4.at[g, core, right]
            wait_here(from_left, l4_recv.at[0, g])
            on = from_left.at[0]
            rcopy(on, on, l4_send.at[2, g], l4_recv.at[2, g], at_ring(right)).start()
            wait_here(from_right, l4_recv.at[1, g])
            on = from_right.at[1]
            rcopy(on, on, l4_send.at[3, g], l4_recv.at[3, g], at_ring(left)).start()

        def share(g):
            across = xg4.at[g, core, lax.rem(ring + 2, nx)]
            wait_here(across.at[0], l4_recv.at[2, g])
            wait_here(across.at[1], l4_recv.at[3, g])
            mine = xg4.at[g, core]
            rcopy(mine, mine, l4_send.at[4, g], l4_recv.at[4, g], (sect, me, ring * 2 + 1 - core)).start()

        def hidden_parts(g):
            wait_here(xg4.at[g, 1 - core], l4_recv.at[4, g])
            pre = jnp.zeros((group_slots, hidden), f32)
            grad = jnp.zeros((group_slots, hidden), f32)
            for q in range(shards):
                cols = slice(q * part, (q + 1) * part)
                pre += dot_nt(xg4[g, q % 2, q // 2, 0], up_ref[:, cols])
                grad += dot_nt(xg4[g, q % 2, q // 2, 1], down_ref[:, cols])
            pre = pre * model_scale
            grad = grad * hidden_scale
            sig = 1.0 / (1.0 + jnp.exp(-pre))
            act_ref[g] = (pre * sig).astype(bf16)
            pre_ref[g] = (grad * sig * (1.0 + pre * (1.0 - sig))).astype(bf16)

        stages = (gather, relay, share, hidden_parts)
        for n in range(GROUPS + len(stages) - 1):
            for stage, run in enumerate(stages):
                if 0 <= n - stage < GROUPS:
                    run(n - stage)

        act = jnp.concatenate([act_ref[g] for g in range(GROUPS)], axis=0)
        pre = jnp.concatenate([pre_ref[g] for g in range(GROUPS)], axis=0)
        for j, (lhs, old, new, scale) in enumerate(
            ((pre, up_ref, fresh_up_ref, model_scale), (act, down_ref, fresh_down_ref, hidden_scale))
        ):
            for q in range(shards):
                cols = slice(q * part, (q + 1) * part)
                rhs = jnp.concatenate([xg4[g, q % 2, q // 2, j] for g in range(GROUPS)], axis=0)
                grad = dot_tn(lhs, rhs) * scale
                new[:, cols] = (old[:, cols].astype(f32) - step_size * grad).astype(bf16)
            rcopy(new, new, fresh_sem.at[j, 0], fresh_sem.at[j, 1], (other, me, dp)).start()

        for i in range(2):
            tables(i, i + 2)
        wait_here(states_ref, st_sem.at[1])
        for i in range(2):
            decode_step(i, i + 2, fresh_up_ref, fresh_down_ref)

        last = states_ref[...].astype(bf16)
        fin_src[...] = jnp.concatenate([last[:dec_rows], last[dec_rows:]], axis=1)
        half = shards // 2
        out_cols = pl.ds(pl.multiple_of(lax.rem(dp, half) * part, part), part)

        @pl.when(dp < half)
        def _():
            def send_far(q, carry):
                to = lax.rem(dp + q, shards)
                rcopy(fin_src, final_ref.at[:, out_cols], fin_sem.at[0], fin_sem.at[1], (other, me, to)).start()
                return carry

            lax.fori_loop(0, shards, send_far, 0)
            wait_here(final_ref, fin_sem.at[1])
            for _ in range(2):
                wait_sent(final_ref, fin_sem.at[0])

        @pl.when(dp >= half)
        def _():
            final_ref[:, out_cols] = fin_src[...]

            def send_near(q, carry):
                to = lax.rem(dp + q, shards)
                rcopy(fin_src, final_ref.at[:, out_cols], fin_sem.at[0], fin_sem.at[1], (sect, me, to)).start()
                return carry

            lax.fori_loop(1, shards, send_near, 0)
            wait_here(final_ref.at[:, pl.ds(0, (half - 1) * part)], fin_sem.at[1])
            wait_sent(final_ref, fin_sem.at[0])
            wait_sent(final_ref.at[:, pl.ds(0, (half - 1) * part)], fin_sem.at[0])

        for i in range(2):
            decode_sent(i)
        wait_sent(out2.at[:, pl.ds(0, experts - 1)], l2_sem.at[0])
        wait_sent(out3.at[:, pl.ds(0, experts - 1)], l3_send)
        for g in range(GROUPS):
            wait_sent(xg4.at[g, core, ring], l4_send.at[0, g])
            wait_sent(xg4.at[g, core, ring], l4_send.at[1, g])
            wait_sent(xg4.at[g, core, ring, 0], l4_send.at[2, g])
            wait_sent(xg4.at[g, core, ring, 1], l4_send.at[3, g])
            wait_sent(xg4.at[g, core], l4_send.at[4, g])
        wait_sent(fresh_up_ref, fresh_sem.at[0, 0])
        wait_sent(fresh_down_ref, fresh_sem.at[1, 0])


def on_device(
    decode_states, norm_gain, decode_routes, decode_gates, up_weight, down_weight,
    traj_inputs, traj_cotangents, traj_lengths, packing, learner_routes, learner_gates,
):
    experts, shards = lax.axis_size("exp"), lax.axis_size("dp")
    dec_rows, width = decode_states.shape
    lrn_rows = learner_routes.shape[0]
    part = width // shards
    hidden = up_weight.shape[2]
    cap_d = 3 * dec_rows * 2 // (2 * experts)
    cap_l = 3 * lrn_rows * 2 // (2 * experts)
    slots = experts * cap_d
    group_slots = experts // GROUPS * cap_l
    half_rows = traj_inputs.shape[1]
    vmem = pl.BlockSpec(memory_space=pltpu.VMEM)
    dma = pltpu.SemaphoreType.DMA
    final, fresh_up, fresh_down = pl.pallas_call(
        functools.partial(kernel, experts, shards, cap_d, cap_l),
        out_shape=(
            jax.ShapeDtypeStruct((dec_rows, width // 2), bf16),
            jax.ShapeDtypeStruct((hidden, width), bf16),
            jax.ShapeDtypeStruct((hidden, width), bf16),
        ),
        in_specs=[vmem] * 15,
        out_specs=(vmem,) * 3,
        scratch_shapes=[
            pltpu.VMEM((2, experts, 8, LANES), bf16),
            pltpu.VMEM((2, experts, 8, LANES), bf16),
            pltpu.VMEM((2, shards, slots, part), bf16),
            pltpu.VMEM((2, shards, slots, part), bf16),
            pltpu.VMEM((2, shards, slots, part), bf16),
            pltpu.VMEM((2, experts, 8, LANES), bf16),
            pltpu.VMEM((2, experts, 8, LANES), bf16),
            pltpu.VMEM((2 * dec_rows, LANES), f32),
            pltpu.VMEM((2, 2, 1, 2 * dec_rows), f32),
            pltpu.VMEM((2, 2, 2 * dec_rows, 1), f32),
            pltpu.VMEM((2, half_rows, part), bf16),
            pltpu.VMEM((2, experts, 8, LANES), bf16),
            pltpu.VMEM((2, experts, 8, LANES), bf16),
            pltpu.VMEM((2, experts, 2 * cap_l, LANES), bf16),
            pltpu.VMEM((2, experts, 2 * cap_l, LANES), bf16),
            pltpu.VMEM((GROUPS, 2, shards // 2, 2, group_slots, part), bf16),
            pltpu.VMEM((GROUPS, group_slots, hidden), bf16),
            pltpu.VMEM((GROUPS, group_slots, hidden), bf16),
            pltpu.VMEM((dec_rows, part), bf16),
            dma((4, 2, 2)),
            dma((2,)),
            dma((2,)),
            dma((2,)),
            dma((2,)),
            dma((2, 2)),
            dma,
            dma((GROUPS,)),
            dma((5, GROUPS)),
            dma((5, GROUPS)),
        ],
        compiler_params=pltpu.CompilerParams(
            collective_id=0, has_side_effects=True, vmem_limit_bytes=48 * 2**20
        ),
    )(
        decode_states, norm_gain.reshape(width // LANES, LANES), decode_routes, decode_gates,
        up_weight[0, 0], down_weight[0, 0], traj_inputs[0], traj_cotangents[0], traj_lengths[0], packing,
        learner_routes, learner_gates, *[jnp.asarray(m) for m in permutations(experts, cap_d, cap_l)],
    )
    return final, fresh_up[None, None], fresh_down[None, None]


def solution(mesh):
    in_specs = (
        P("exp", None),
        P(),
        P(None, "exp", None),
        P(None, "exp", None),
        P("sect", "exp", "dp", None),
        P("sect", "exp", "dp", None),
        P("sect", "exp", None),
        P("sect", "exp", None),
        P("exp", None, None),
        P("exp", None),
        P("exp", None),
        P("exp", None),
    )
    out_specs = (P("exp", "sect"), P("sect", "exp", "dp", None), P("sect", "exp", "dp", None))
    return jax.shard_map(on_device, mesh=mesh, in_specs=in_specs, out_specs=out_specs, check_vma=False)
```

```python
import functools

import jax
import jax.numpy as jnp
from jax import lax
from jax.experimental import pallas as pl
from jax.experimental.pallas import tpu as pltpu
from jax.sharding import PartitionSpec as P

MESH = pl.DeviceIdType.MESH
step_size = 3.0
norm_eps = 1e-06
f32 = jnp.float32
bf16 = jnp.bfloat16
LANES = 128
GROUPS = 4


def dot(a, b):
    return lax.dot_general(a, b, (((1,), (0,)), ((), ())), preferred_element_type=f32)


def dot_nt(a, b):
    return lax.dot_general(a, b, (((1,), (1,)), ((), ())), preferred_element_type=f32)


def dot_tn(a, b):
    return lax.dot_general(a, b, (((0,), (0,)), ((), ())), preferred_element_type=f32)


def iota(shape, dim):
    return lax.broadcasted_iota(jnp.int32, shape, dim).astype(f32)


def to_row(col):
    n = col.shape[0]
    eye = iota((n, n), 0) == iota((n, n), 1)
    return jnp.sum(jnp.where(eye, col, 0.0), axis=0, keepdims=True)


def to_col(row):
    n = row.shape[1]
    eye = iota((n, n), 0) == iota((n, n), 1)
    return jnp.sum(jnp.where(eye, row, 0.0), axis=1, keepdims=True)


def ranks(first, second):
    n = first.shape[0]
    first_row, second_row = to_row(first), to_row(second)
    before = iota((n, n), 1) < iota((n, n), 0)
    out = []
    for mine in (first, second):
        same = ((first_row == mine) | (second_row == mine)) & before
        out.append(jnp.sum(jnp.where(same, 1.0, 0.0), axis=1, keepdims=True))
    return out


def far_first(count):
    return sorted(range(1, count), key=lambda k: (-min(k, count - k), k))


def slot_place(slot, per_source, block, c, half_step):
    source = jnp.floor((slot + 0.5) * (1.0 / per_source))
    return source * block + c * half_step + (slot - source * per_source)


def ones_where(condition):
    return jnp.where(condition, 1.0, 0.0).astype(bf16)


def kernel(
    experts, shards, cap_d, cap_l,
    rows_ref, gain_ref, routes_ref, gates_ref, up_ref, down_ref, in_ref, cot_ref, len_ref, pack_ref,
    lroutes_ref, lgates_ref,
    final_ref, fresh_up_ref, fresh_down_ref,
    d1_out, d1_in, xg, d3_out, d3_in, d4_out, d4_in, states_ref, trow_ref, tcol_ref, gcol_ref,
    held, out2, recv2, out3, recv3, xg4, act_ref, pre_ref, fin_src,
    up_v, down_v, rows_v, own_v, take_d, give_d, take_l,
    load_sem, dec_send, ends_recv, half_recv, l1_sem, l2_sem, st_sem, fin_sem, fresh_sem, l3_send, l3_recv, l4_send, l4_recv,
):
    sect, me, dp = lax.axis_index("sect"), lax.axis_index("exp"), lax.axis_index("dp")
    ring, core = lax.div(dp, 2), lax.rem(dp, 2)
    other = 1 - sect
    width = rows_ref.shape[1]
    part = width // shards
    hidden = up_ref.shape[0]
    model_scale = width ** (-0.5)
    hidden_scale = (hidden * shards) ** (-0.5)
    dec_rows = rows_ref.shape[0]
    slots = experts * cap_d
    per = experts // GROUPS
    group_slots = per * cap_l
    col0 = pl.multiple_of(dp * part, part)
    low, half = experts // 4, experts // 2
    half_slots = half * cap_d
    sect_far_first = far_first(experts)
    loads = [
        pltpu.make_async_copy(rows_ref.at[:, pl.ds(col0, part)], rows_v, load_sem.at[0]),
        pltpu.make_async_copy(in_ref.at[:, pl.ds(col0, part)], own_v.at[0], load_sem.at[1]),
        pltpu.make_async_copy(cot_ref.at[:, pl.ds(col0, part)], own_v.at[1], load_sem.at[2]),
        pltpu.make_async_copy(up_ref, up_v, load_sem.at[3]),
        pltpu.make_async_copy(down_ref, down_v, load_sem.at[4]),
    ]

    def rcopy(src, dst, send, recv, device):
        return pltpu.make_async_remote_copy(
            src_ref=src, dst_ref=dst, send_sem=send, recv_sem=recv, device_id=device, device_id_type=MESH
        )

    def wait_sent(ref, sem):
        rcopy(ref, ref, sem, sem, (sect, me, dp)).wait_send()

    def wait_here(ref, sem):
        rcopy(ref, ref, sem, sem, (sect, me, dp)).wait_recv()

    barrier = pltpu.get_barrier_semaphore()

    for k in sect_far_first:
        pl.semaphore_signal(barrier, inc=1, device_id=(sect, lax.rem(me + k, experts), dp), device_id_type=MESH)
    for q in range(1, shards):
        pl.semaphore_signal(barrier, inc=1, device_id=(sect, me, lax.rem(dp + q, shards)), device_id_type=MESH)
    for q in range(shards):
        pl.semaphore_signal(barrier, inc=1, device_id=(other, me, lax.rem(dp + q, shards)), device_id_type=MESH)
    for load in loads:
        load.start()
    for c in range(2):
        row, col = iota((half_slots, half * 8), 0), iota((half_slots, half * 8), 1)
        take_d[c] = ones_where(col == slot_place(row, cap_d, 8.0, c, 4.0))
        row, col = iota((half * 8, half_slots), 0), iota((half * 8, half_slots), 1)
        give_d[c] = ones_where(row == slot_place(col, cap_d, 8.0, c, 4.0))
        row, col = iota((group_slots, 2 * group_slots), 0), iota((group_slots, 2 * group_slots), 1)
        take_l[c] = ones_where(col == slot_place(row, cap_l, 2.0 * cap_l, c, float(cap_l)))

    def greeted():
        pl.semaphore_wait(barrier, experts - 1 + shards - 1 + shards)

    def tables(i, t):
        routes = routes_ref[t].astype(f32)
        first, second = to_col(routes[0:1]), to_col(routes[1:2])
        within = ranks(first, second)
        for k, mine in enumerate((first, second)):
            target = mine * 8.0 + within[k]
            both = jnp.concatenate([target, target + 4.0], axis=0)
            tcol_ref[i, k] = both
            trow_ref[i, k] = to_row(both)
        for k in range(2):
            gate = to_col(gates_ref[t, k : k + 1, :])
            gcol_ref[i, k] = jnp.concatenate([gate, gate], axis=0)

    def decode_step(i, t, up, down):
        gain0, gain1 = gain_ref[pl.ds(2 * dp, 1), :], gain_ref[pl.ds(2 * dp + 1, 1), :]
        gains = jnp.concatenate(
            [jnp.broadcast_to(gain0, (dec_rows, LANES)), jnp.broadcast_to(gain1, (dec_rows, LANES))], axis=0
        )
        y = (states_ref[...] * gains).astype(bf16)
        row_ids = iota((experts * 8, 2 * dec_rows), 0)
        pick = (row_ids == trow_ref[i, 0]) | (row_ids == trow_ref[i, 1])
        pick = jnp.where(pick, 1.0, 0.0).astype(bf16)
        d1_out[i] = dot(pick, y).astype(bf16).reshape(experts, 8, LANES)
        for k in sect_far_first:
            place = (k - low) % experts
            to = lax.rem(me + k, experts)
            arrival = half_recv.at[0, i, place // half]
            rcopy(d1_out.at[i, to], d1_in.at[i, place], dec_send.at[0, i], arrival, (sect, to, dp)).start()
        own_place = experts - low
        d1_in[i, own_place] = d1_out[i, me]

        def gather(h):
            wait_here(d1_in.at[i, pl.ds(h * half, half - h)], half_recv.at[0, i, h])
            arrived = d1_in[i, h * half : (h + 1) * half].reshape(half * 8, LANES)
            block = [dot(take_d[c], arrived).astype(bf16) for c in range(2)]
            xg[i, h, dp] = jnp.concatenate(block, axis=1)
            mine = xg.at[i, h, dp]
            for q in far_first(shards):
                to = lax.rem(dp + q, shards)
                rcopy(mine, mine, dec_send.at[1 + h, i], half_recv.at[1, i, h], (sect, me, to)).start()

        def up_part(h):
            wait_here(xg.at[i, h, pl.ds(0, shards - 1)], half_recv.at[1, i, h])
            before_act = jnp.zeros((half_slots, hidden), f32)
            squares = jnp.zeros((half_slots, part), f32)
            for q in range(shards):
                piece = xg[i, h, q]
                before_act += dot_nt(piece, up[:, q * part : (q + 1) * part])
                gain = jnp.concatenate([gain_ref[2 * q : 2 * q + 1], gain_ref[2 * q + 1 : 2 * q + 2]], axis=1)
                wide = piece.astype(f32) * (1.0 / gain)
                squares += wide * wide
            mean = jnp.sum(squares, axis=1, keepdims=True) * (1.0 / width)
            before_act = before_act * (lax.rsqrt(mean + norm_eps) * model_scale)
            return (before_act / (1.0 + jnp.exp(-before_act))).astype(bf16)

        def down_part(h, act):
            for q in range(shards):
                d3_out[i, h, q] = (dot(act, down[:, q * part : (q + 1) * part]) * hidden_scale).astype(bf16)
            for q in far_first(shards):
                to = lax.rem(dp + q, shards)
                rcopy(
                    d3_out.at[i, h, to], d3_in.at[i, h, dp], dec_send.at[3 + h, i], half_recv.at[2, i, h], (sect, me, to)
                ).start()
            d3_in[i, h, dp] = d3_out[i, h, dp]

        def give_back(h):
            wait_here(d3_in.at[i, h, pl.ds(0, shards - 1)], half_recv.at[2, i, h])
            total = d3_in[i, h, 0].astype(f32)
            for q in range(1, shards):
                total += d3_in[i, h, q].astype(f32)
            total = total.astype(bf16)
            back = dot(give_d[0], total[:, :LANES]) + dot(give_d[1], total[:, LANES:])
            d4_out[i, h * half : (h + 1) * half] = back.astype(bf16).reshape(half, 8, LANES)
            for k in sect_far_first:
                place = (k - low) % experts
                if place // half == h:
                    to = lax.rem(me + experts - k, experts)
                    rcopy(d4_out.at[i, place], d4_in.at[i, me], dec_send.at[5, i], ends_recv.at[i], (sect, to, dp)).start()

        gather(1)
        gather(0)
        near_act = up_part(1)
        down_part(0, up_part(0))
        down_part(1, near_act)
        give_back(0)
        give_back(1)
        d4_in[i, me] = d4_out[i, own_place]
        lane_ids = iota((2 * dec_rows, experts * 8), 1)
        mix = jnp.where(lane_ids == tcol_ref[i, 0], gcol_ref[i, 0], 0.0)
        mix += jnp.where(lane_ids == tcol_ref[i, 1], gcol_ref[i, 1], 0.0)
        high = mix.astype(bf16)
        rest = mix - high.astype(f32)
        middle = rest.astype(bf16)
        low_part = (rest - middle.astype(f32)).astype(bf16)
        wait_here(d4_in.at[i, pl.ds(0, experts - 1)], ends_recv.at[i])
        returned = d4_in[i].reshape(experts * 8, LANES)
        states_ref[...] += dot(high, returned) + (dot(middle, returned) + dot(low_part, returned))

    def decode_sent(i):
        wait_sent(d1_out.at[i, pl.ds(0, experts - 1)], dec_send.at[0, i])
        for h in range(2):
            wait_sent(xg.at[i, h, pl.ds(0, shards - 1)], dec_send.at[1 + h, i])
            wait_sent(d3_out.at[i, h, pl.ds(0, shards - 1)], dec_send.at[3 + h, i])
        wait_sent(d4_out.at[i, pl.ds(0, experts - 1)], dec_send.at[5, i])

    @pl.when(sect == 0)
    def _():
        for i in range(2):
            tables(i, i)
        loads[0].wait()
        rows = rows_v[...].astype(f32)
        states_ref[...] = jnp.concatenate([rows[:, :LANES], rows[:, LANES:]], axis=0)
        loads[1].wait()
        loads[2].wait()
        greeted()
        rcopy(own_v, held, l1_sem.at[0], l1_sem.at[1], (other, me, dp)).start()
        loads[3].wait()
        loads[4].wait()
        for i in range(2):
            decode_step(i, i, up_v, down_v)
        move = rcopy(states_ref, states_ref, st_sem.at[0], st_sem.at[1], (other, me, dp))
        move.start()
        move.wait_send()
        wait_sent(held, l1_sem.at[0])
        for i in range(2):
            decode_sent(i)
        wait_here(fresh_up_ref, fresh_sem.at[0, 1])
        wait_here(fresh_down_ref, fresh_sem.at[1, 1])
        wait_here(final_ref, fin_sem.at[1])

    @pl.when(sect == 1)
    def _():
        lengths = len_ref[...].astype(f32)
        count = lengths.shape[1]
        length = jnp.concatenate([to_col(lengths[0:1]), to_col(lengths[1:2])], axis=0)
        both = 2 * count
        a, b = iota((both, both), 0), iota((both, both), 1)
        same_half = (a < count) == (b < count)
        start_row = jnp.sum(jnp.where(same_half & (a < b), length, 0.0), axis=0, keepdims=True)
        length_row = to_row(length)
        half_rows = held.shape[1]
        r, t = iota((2 * half_rows, both), 0), iota((2 * half_rows, both), 1)
        second = r >= half_rows
        row_in = r - jnp.where(second, float(half_rows), 0.0)
        offset = row_in - start_row
        inside = (second == (t >= count)) & (offset >= 0.0) & (offset < length_row)
        shard = pack_ref[...].astype(f32)
        target2 = jnp.sum(jnp.where(inside, shard * 8.0 + offset, 0.0), axis=1, keepdims=True)
        target2 = to_row(jnp.concatenate([target2, target2 + 4.0], axis=0))
        row_ids = iota((experts * 8, 4 * half_rows), 0)
        pack = ones_where(row_ids == target2)
        for load in loads:
            load.wait()
        for i in range(2):
            tables(i, i + 2)
        greeted()
        wait_here(held, l1_sem.at[1])
        for j in range(2):
            far, own = held[j], own_v[j]
            stacked = jnp.concatenate([far[:, :LANES], own[:, :LANES], far[:, LANES:], own[:, LANES:]], axis=0)
            out2[j] = dot(pack, stacked).astype(bf16).reshape(experts, 8, LANES)
            recv2[j, me] = out2[j, me]

        for k in sect_far_first:
            to = lax.rem(me + k, experts)
            rcopy(out2.at[:, to], recv2.at[:, me], l2_sem.at[0], l2_sem.at[1], (sect, to, dp)).start()

        lroutes = lroutes_ref[...].astype(f32)
        first, second = to_col(lroutes[0:1]), to_col(lroutes[1:2])
        within = ranks(first, second)
        gates = [to_col(lgates_ref[k : k + 1, :]) for k in range(2)]

        def by_half(col, step):
            n = col.shape[0]
            row = jnp.zeros((1, 2 * n), f32)
            r, l = iota((n, 2 * n), 0), iota((n, 2 * n), 1)
            source = jnp.floor(r * 0.25)
            place = source * 4.0 + r
            row += jnp.sum(jnp.where(l == place, col, 0.0), axis=0, keepdims=True)
            row += jnp.sum(jnp.where(l == place + 4.0, col + step, 0.0), axis=0, keepdims=True)
            return row

        stride = 2.0 * cap_l
        tr0 = by_half(first * stride + within[0], float(cap_l))
        tr1 = by_half(second * stride + within[1], float(cap_l))
        gr0, gr1 = by_half(gates[0], 0.0), by_half(gates[1], 0.0)
        ids = iota((experts * 2 * cap_l, experts * 8), 0)
        hit0, hit1 = ids == tr0, ids == tr1
        pick = ones_where(hit0 | hit1)
        scale = jnp.where(hit0, gr0, 0.0) + jnp.where(hit1, gr1, 0.0)
        high = scale.astype(bf16)
        low = (scale - high.astype(f32)).astype(bf16)
        wait_here(recv2.at[:, pl.ds(0, experts - 1)], l2_sem.at[1])
        inputs = recv2[0].reshape(experts * 8, LANES)
        cots = recv2[1].reshape(experts * 8, LANES)
        out3[0] = dot(pick, inputs).astype(bf16).reshape(experts, 2 * cap_l, LANES)
        out3[1] = (dot(high, cots) + dot(low, cots)).astype(bf16).reshape(experts, 2 * cap_l, LANES)
        for g in range(GROUPS):
            for k in sect_far_first:
                if k % GROUPS == g:
                    to = lax.rem(me + k, experts)
                    place = g * per + k // GROUPS
                    rcopy(out3.at[:, to], recv3.at[:, place], l3_send, l3_recv.at[g], (sect, to, dp)).start()
        recv3[0, 0] = out3[0, me]
        recv3[1, 0] = out3[1, me]

        nx = shards // 2
        right, left = lax.rem(ring + 1, nx), lax.rem(ring + nx - 1, nx)

        def at_ring(position):
            return (sect, me, position * 2 + core)

        def spread(g):
            first_in = 1 if g == 0 else 0
            if per - first_in:
                wait_here(recv3.at[:, pl.ds(g * per + first_in, per - first_in)], l3_recv.at[g])
            for j in range(2):
                rows = recv3[j, g * per : (g + 1) * per].reshape(per * 2 * cap_l, LANES)
                block = [dot(take_l[c], rows).astype(bf16) for c in range(2)]
                xg4[g, core, ring, j] = jnp.concatenate(block, axis=1)
            mine = xg4.at[g, core, ring]
            rcopy(mine, mine, l4_send.at[0, g], l4_recv.at[0, g], at_ring(right)).start()
            rcopy(mine, mine, l4_send.at[1, g], l4_recv.at[1, g], at_ring(left)).start()

        def relay(g):
            from_left, from_right = xg4.at[g, core, left], xg4.at[g, core, right]
            wait_here(from_left, l4_recv.at[0, g])
            on = from_left.at[0]
            rcopy(on, on, l4_send.at[2, g], l4_recv.at[2, g], at_ring(right)).start()
            wait_here(from_right, l4_recv.at[1, g])
            on = from_right.at[1]
            rcopy(on, on, l4_send.at[3, g], l4_recv.at[3, g], at_ring(left)).start()

        def share(g):
            across = xg4.at[g, core, lax.rem(ring + 2, nx)]
            wait_here(across.at[0], l4_recv.at[2, g])
            wait_here(across.at[1], l4_recv.at[3, g])
            mine = xg4.at[g, core]
            rcopy(mine, mine, l4_send.at[4, g], l4_recv.at[4, g], (sect, me, ring * 2 + 1 - core)).start()

        def hidden_parts(g):
            wait_here(xg4.at[g, 1 - core], l4_recv.at[4, g])
            pre = jnp.zeros((group_slots, hidden), f32)
            grad = jnp.zeros((group_slots, hidden), f32)
            for q in range(shards):
                cols = slice(q * part, (q + 1) * part)
                pre += dot_nt(xg4[g, q % 2, q // 2, 0], up_v[:, cols])
                grad += dot_nt(xg4[g, q % 2, q // 2, 1], down_v[:, cols])
            pre = pre * model_scale
            grad = grad * hidden_scale
            sig = 1.0 / (1.0 + jnp.exp(-pre))
            act_ref[g] = (pre * sig).astype(bf16)
            pre_ref[g] = (grad * sig * (1.0 + pre * (1.0 - sig))).astype(bf16)

        stages = (spread, relay, share, hidden_parts)
        for n in range(GROUPS + len(stages) - 1):
            for stage, run in enumerate(stages):
                if 0 <= n - stage < GROUPS:
                    run(n - stage)

        act = jnp.concatenate([act_ref[g] for g in range(GROUPS)], axis=0)
        pre = jnp.concatenate([pre_ref[g] for g in range(GROUPS)], axis=0)
        for j, (lhs, old, new, scale) in enumerate(
            ((pre, up_v, fresh_up_ref, model_scale), (act, down_v, fresh_down_ref, hidden_scale))
        ):
            for q in range(shards):
                cols = slice(q * part, (q + 1) * part)
                rhs = jnp.concatenate([xg4[g, q % 2, q // 2, j] for g in range(GROUPS)], axis=0)
                grad = dot_tn(lhs, rhs) * scale
                new[:, cols] = (old[:, cols].astype(f32) - step_size * grad).astype(bf16)
            rcopy(new, new, fresh_sem.at[j, 0], fresh_sem.at[j, 1], (other, me, dp)).start()

        wait_here(states_ref, st_sem.at[1])
        for i in range(2):
            decode_step(i, i + 2, fresh_up_ref, fresh_down_ref)

        last = states_ref[...].astype(bf16)
        fin_src[...] = jnp.concatenate([last[:dec_rows], last[dec_rows:]], axis=1)
        near = shards // 2
        out_cols = pl.ds(pl.multiple_of(lax.rem(dp, near) * part, part), part)

        @pl.when(dp < near)
        def _():
            def send_far(q, carry):
                to = lax.rem(dp + q, shards)
                rcopy(fin_src, final_ref.at[:, out_cols], fin_sem.at[0], fin_sem.at[1], (other, me, to)).start()
                return carry

            lax.fori_loop(0, shards, send_far, 0)
            wait_here(final_ref, fin_sem.at[1])
            for _ in range(2):
                wait_sent(final_ref, fin_sem.at[0])

        @pl.when(dp >= near)
        def _():
            final_ref[:, out_cols] = fin_src[...]

            def send_near(q, carry):
                to = lax.rem(dp + q, shards)
                rcopy(fin_src, final_ref.at[:, out_cols], fin_sem.at[0], fin_sem.at[1], (sect, me, to)).start()
                return carry

            lax.fori_loop(1, shards, send_near, 0)
            wait_here(final_ref.at[:, pl.ds(0, (near - 1) * part)], fin_sem.at[1])
            wait_sent(final_ref, fin_sem.at[0])
            wait_sent(final_ref.at[:, pl.ds(0, (near - 1) * part)], fin_sem.at[0])

        for i in range(2):
            decode_sent(i)
        wait_sent(out2.at[:, pl.ds(0, experts - 1)], l2_sem.at[0])
        wait_sent(out3.at[:, pl.ds(0, experts - 1)], l3_send)
        for g in range(GROUPS):
            wait_sent(xg4.at[g, core, ring], l4_send.at[0, g])
            wait_sent(xg4.at[g, core, ring], l4_send.at[1, g])
            wait_sent(xg4.at[g, core, ring, 0], l4_send.at[2, g])
            wait_sent(xg4.at[g, core, ring, 1], l4_send.at[3, g])
            wait_sent(xg4.at[g, core], l4_send.at[4, g])
        wait_sent(fresh_up_ref, fresh_sem.at[0, 0])
        wait_sent(fresh_down_ref, fresh_sem.at[1, 0])


def on_device(
    decode_states, norm_gain, decode_routes, decode_gates, up_weight, down_weight,
    traj_inputs, traj_cotangents, traj_lengths, packing, learner_routes, learner_gates,
):
    experts, shards = lax.axis_size("exp"), lax.axis_size("dp")
    dec_rows, width = decode_states.shape
    lrn_rows = learner_routes.shape[0]
    part = width // shards
    hidden = up_weight.shape[2]
    cap_d = 3 * dec_rows * 2 // (2 * experts)
    cap_l = 3 * lrn_rows * 2 // (2 * experts)
    slots = experts * cap_d
    group_slots = experts // GROUPS * cap_l
    half_rows = traj_inputs.shape[1]
    vmem = pl.BlockSpec(memory_space=pltpu.VMEM)
    hbm = pl.BlockSpec(memory_space=pltpu.HBM)
    dma = pltpu.SemaphoreType.DMA
    final, fresh_up, fresh_down = pl.pallas_call(
        functools.partial(kernel, experts, shards, cap_d, cap_l),
        out_shape=(
            jax.ShapeDtypeStruct((dec_rows, width // 2), bf16),
            jax.ShapeDtypeStruct((hidden, width), bf16),
            jax.ShapeDtypeStruct((hidden, width), bf16),
        ),
        in_specs=[hbm, vmem, vmem, vmem, hbm, hbm, hbm, hbm, vmem, vmem, vmem, vmem],
        out_specs=(vmem,) * 3,
        scratch_shapes=[
            pltpu.VMEM((2, experts, 8, LANES), bf16),
            pltpu.VMEM((2, experts, 8, LANES), bf16),
            pltpu.VMEM((2, 2, shards, slots // 2, part), bf16),
            pltpu.VMEM((2, 2, shards, slots // 2, part), bf16),
            pltpu.VMEM((2, 2, shards, slots // 2, part), bf16),
            pltpu.VMEM((2, experts, 8, LANES), bf16),
            pltpu.VMEM((2, experts, 8, LANES), bf16),
            pltpu.VMEM((2 * dec_rows, LANES), f32),
            pltpu.VMEM((2, 2, 1, 2 * dec_rows), f32),
            pltpu.VMEM((2, 2, 2 * dec_rows, 1), f32),
            pltpu.VMEM((2, 2, 2 * dec_rows, 1), f32),
            pltpu.VMEM((2, half_rows, part), bf16),
            pltpu.VMEM((2, experts, 8, LANES), bf16),
            pltpu.VMEM((2, experts, 8, LANES), bf16),
            pltpu.VMEM((2, experts, 2 * cap_l, LANES), bf16),
            pltpu.VMEM((2, experts, 2 * cap_l, LANES), bf16),
            pltpu.VMEM((GROUPS, 2, shards // 2, 2, group_slots, part), bf16),
            pltpu.VMEM((GROUPS, group_slots, hidden), bf16),
            pltpu.VMEM((GROUPS, group_slots, hidden), bf16),
            pltpu.VMEM((dec_rows, part), bf16),
            pltpu.VMEM((hidden, width), bf16),
            pltpu.VMEM((hidden, width), bf16),
            pltpu.VMEM((dec_rows, part), bf16),
            pltpu.VMEM((2, half_rows, part), bf16),
            pltpu.VMEM((2, slots // 2, experts * 4), bf16),
            pltpu.VMEM((2, experts * 4, slots // 2), bf16),
            pltpu.VMEM((2, group_slots, 2 * group_slots), bf16),
            dma((5,)),
            dma((6, 2)),
            dma((2,)),
            dma((3, 2, 2)),
            dma((2,)),
            dma((2,)),
            dma((2,)),
            dma((2,)),
            dma((2, 2)),
            dma,
            dma((GROUPS,)),
            dma((5, GROUPS)),
            dma((5, GROUPS)),
        ],
        compiler_params=pltpu.CompilerParams(
            collective_id=0, has_side_effects=True, vmem_limit_bytes=56 * 2**20
        ),
    )(
        decode_states, norm_gain.reshape(width // LANES, LANES),
        decode_routes.transpose(0, 2, 1), decode_gates.transpose(0, 2, 1),
        up_weight[0, 0], down_weight[0, 0], traj_inputs[0], traj_cotangents[0], traj_lengths[0], packing,
        learner_routes.T, learner_gates.T,
    )
    return final, fresh_up[None, None], fresh_down[None, None]


def solution(mesh):
    in_specs = (
        P("exp", None),
        P(),
        P(None, "exp", None),
        P(None, "exp", None),
        P("sect", "exp", "dp", None),
        P("sect", "exp", "dp", None),
        P("sect", "exp", None),
        P("sect", "exp", None),
        P("exp", None, None),
        P("exp", None),
        P("exp", None),
        P("exp", None),
    )
    out_specs = (P("exp", "sect"), P("sect", "exp", "dp", None), P("sect", "exp", "dp", None))
    return jax.shard_map(on_device, mesh=mesh, in_specs=in_specs, out_specs=out_specs, check_vma=False)
```

```python
import functools

import jax
import jax.numpy as jnp
from jax import lax
from jax.experimental import pallas as pl
from jax.experimental.pallas import tpu as pltpu
from jax.sharding import PartitionSpec as P

MESH = pl.DeviceIdType.MESH
step_size = 3.0
norm_eps = 1e-06
f32 = jnp.float32
bf16 = jnp.bfloat16
LANES = 128
GROUPS = 4


def dot(a, b):
    return lax.dot_general(a, b, (((1,), (0,)), ((), ())), preferred_element_type=f32)


def dot_nt(a, b):
    return lax.dot_general(a, b, (((1,), (1,)), ((), ())), preferred_element_type=f32)


def dot_tn(a, b):
    return lax.dot_general(a, b, (((0,), (0,)), ((), ())), preferred_element_type=f32)


def iota(shape, dim):
    return lax.broadcasted_iota(jnp.int32, shape, dim).astype(f32)


def to_row(col):
    n = col.shape[0]
    eye = iota((n, n), 0) == iota((n, n), 1)
    return jnp.sum(jnp.where(eye, col, 0.0), axis=0, keepdims=True)


def to_col(row):
    n = row.shape[1]
    eye = iota((n, n), 0) == iota((n, n), 1)
    return jnp.sum(jnp.where(eye, row, 0.0), axis=1, keepdims=True)


def ranks(first, second):
    n = first.shape[0]
    first_row, second_row = to_row(first), to_row(second)
    before = iota((n, n), 1) < iota((n, n), 0)
    out = []
    for mine in (first, second):
        same = ((first_row == mine) | (second_row == mine)) & before
        out.append(jnp.sum(jnp.where(same, 1.0, 0.0), axis=1, keepdims=True))
    return out


def far_first(count):
    return sorted(range(1, count), key=lambda k: (-min(k, count - k), k))


def slot_place(slot, per_source, block, c, half_step):
    source = jnp.floor((slot + 0.5) * (1.0 / per_source))
    return source * block + c * half_step + (slot - source * per_source)


def ones_where(condition):
    return jnp.where(condition, 1.0, 0.0).astype(bf16)


def kernel(
    experts, shards, cap_d, cap_l,
    rows_ref, gain_ref, routes_ref, gates_ref, up_ref, down_ref, in_ref, cot_ref, len_ref, pack_ref,
    lroutes_ref, lgates_ref,
    final_ref, fresh_up_ref, fresh_down_ref,
    d1_out, d1_in, xg_far, xg_near, d3_out_far, d3_out_near, d3_in_far, d3_in_near, d4_out, d4_in, states_ref, trow_ref, tcol_ref, gcol_ref,
    held, out2, recv2, out3, recv3, xg4, act_ref, pre_ref, fin_src,
    up_v, down_v, rows_v, own_v, take_far, take_near, give_far, give_near, take_l,
    load_sem, dec_send, ends_recv, half_recv, l1_sem, l2_sem, st_sem, fin_sem, fresh_sem, l3_send, l3_recv, l4_send, l4_recv,
):
    sect, me, dp = lax.axis_index("sect"), lax.axis_index("exp"), lax.axis_index("dp")
    ring, core = lax.div(dp, 2), lax.rem(dp, 2)
    other = 1 - sect
    width = rows_ref.shape[1]
    part = width // shards
    hidden = up_ref.shape[0]
    model_scale = width ** (-0.5)
    hidden_scale = (hidden * shards) ** (-0.5)
    dec_rows = rows_ref.shape[0]
    per = experts // GROUPS
    group_slots = per * cap_l
    col0 = pl.multiple_of(dp * part, part)
    sizes = (experts // 4, experts - experts // 4)
    firsts = (0, sizes[0])
    low = (experts - sizes[0] + 1) // 2
    xg, d3_out, d3_in = (xg_far, xg_near), (d3_out_far, d3_out_near), (d3_in_far, d3_in_near)
    take_d, give_d = (take_far, take_near), (give_far, give_near)
    sect_far_first = far_first(experts)
    loads = [
        pltpu.make_async_copy(rows_ref.at[:, pl.ds(col0, part)], rows_v, load_sem.at[0]),
        pltpu.make_async_copy(in_ref.at[:, pl.ds(col0, part)], own_v.at[0], load_sem.at[1]),
        pltpu.make_async_copy(cot_ref.at[:, pl.ds(col0, part)], own_v.at[1], load_sem.at[2]),
        pltpu.make_async_copy(up_ref, up_v, load_sem.at[3]),
        pltpu.make_async_copy(down_ref, down_v, load_sem.at[4]),
    ]

    def rcopy(src, dst, send, recv, device):
        return pltpu.make_async_remote_copy(
            src_ref=src, dst_ref=dst, send_sem=send, recv_sem=recv, device_id=device, device_id_type=MESH
        )

    def wait_sent(ref, sem):
        rcopy(ref, ref, sem, sem, (sect, me, dp)).wait_send()

    def wait_here(ref, sem):
        rcopy(ref, ref, sem, sem, (sect, me, dp)).wait_recv()

    barrier = pltpu.get_barrier_semaphore()

    for k in sect_far_first:
        pl.semaphore_signal(barrier, inc=1, device_id=(sect, lax.rem(me + k, experts), dp), device_id_type=MESH)
    for k in sect_far_first:
        pl.semaphore_signal(barrier, inc=1, device_id=(other, lax.rem(me + k, experts), dp), device_id_type=MESH)
    for q in range(1, shards):
        pl.semaphore_signal(barrier, inc=1, device_id=(sect, me, lax.rem(dp + q, shards)), device_id_type=MESH)
    for q in range(shards):
        pl.semaphore_signal(barrier, inc=1, device_id=(other, me, lax.rem(dp + q, shards)), device_id_type=MESH)
    for load in loads:
        load.start()
    for c in range(2):
        for h, size in enumerate(sizes):
            row, col = iota((size * cap_d, size * 8), 0), iota((size * cap_d, size * 8), 1)
            take_d[h][c] = ones_where(col == slot_place(row, cap_d, 8.0, c, 4.0))
            row, col = iota((size * 8, size * cap_d), 0), iota((size * 8, size * cap_d), 1)
            give_d[h][c] = ones_where(row == slot_place(col, cap_d, 8.0, c, 4.0))
        row, col = iota((group_slots, 2 * group_slots), 0), iota((group_slots, 2 * group_slots), 1)
        take_l[c] = ones_where(col == slot_place(row, cap_l, 2.0 * cap_l, c, float(cap_l)))

    def greeted():
        pl.semaphore_wait(barrier, 2 * (experts - 1) + shards - 1 + shards)

    def tables(i, t):
        routes = routes_ref[t].astype(f32)
        first, second = to_col(routes[0:1]), to_col(routes[1:2])
        within = ranks(first, second)
        for k, mine in enumerate((first, second)):
            target = mine * 8.0 + within[k]
            both = jnp.concatenate([target, target + 4.0], axis=0)
            tcol_ref[i, k] = both
            trow_ref[i, k] = to_row(both)
        for k in range(2):
            gate = to_col(gates_ref[t, k : k + 1, :])
            gcol_ref[i, k] = jnp.concatenate([gate, gate], axis=0)

    def decode_step(i, up, down, meanwhile=None, hand_over=False):
        gain0, gain1 = gain_ref[pl.ds(2 * dp, 1), :], gain_ref[pl.ds(2 * dp + 1, 1), :]
        gains = jnp.concatenate(
            [jnp.broadcast_to(gain0, (dec_rows, LANES)), jnp.broadcast_to(gain1, (dec_rows, LANES))], axis=0
        )
        y = (states_ref[...] * gains).astype(bf16)
        row_ids = iota((experts * 8, 2 * dec_rows), 0)
        pick = (row_ids == trow_ref[i, 0]) | (row_ids == trow_ref[i, 1])
        pick = jnp.where(pick, 1.0, 0.0).astype(bf16)
        d1_out[i] = dot(pick, y).astype(bf16).reshape(experts, 8, LANES)
        for k in sect_far_first:
            place = (k - low) % experts
            to = lax.rem(me + k, experts)
            arrival = half_recv.at[0, i, 0 if place < sizes[0] else 1]
            rcopy(d1_out.at[i, to], d1_in.at[i, place], dec_send.at[0, i], arrival, (sect, to, dp)).start()
        own_place = experts - low
        d1_in[i, own_place] = d1_out[i, me]

        def gather(h):
            first, size = firsts[h], sizes[h]
            wait_here(d1_in.at[i, pl.ds(first, size - h)], half_recv.at[0, i, h])
            arrived = d1_in[i, first : first + size].reshape(size * 8, LANES)
            block = [dot(take_d[h][c], arrived).astype(bf16) for c in range(2)]
            xg[h][i, dp] = jnp.concatenate(block, axis=1)
            mine = xg[h].at[i, dp]
            for q in far_first(shards):
                to = lax.rem(dp + q, shards)
                rcopy(mine, mine, dec_send.at[1 + h, i], half_recv.at[1, i, h], (sect, me, to)).start()

        def up_part(h):
            wait_here(xg[h].at[i, pl.ds(0, shards - 1)], half_recv.at[1, i, h])
            before_act = jnp.zeros((sizes[h] * cap_d, hidden), f32)
            squares = jnp.zeros((sizes[h] * cap_d, part), f32)
            for q in range(shards):
                piece = xg[h][i, q]
                before_act += dot_nt(piece, up[:, q * part : (q + 1) * part])
                gain = jnp.concatenate([gain_ref[2 * q : 2 * q + 1], gain_ref[2 * q + 1 : 2 * q + 2]], axis=1)
                wide = piece.astype(f32) * (1.0 / gain)
                squares += wide * wide
            mean = jnp.sum(squares, axis=1, keepdims=True) * (1.0 / width)
            before_act = before_act * (lax.rsqrt(mean + norm_eps) * model_scale)
            return (before_act / (1.0 + jnp.exp(-before_act))).astype(bf16)

        def down_part(h, act):
            for q in range(shards):
                d3_out[h][i, q] = (dot(act, down[:, q * part : (q + 1) * part]) * hidden_scale).astype(bf16)
            for q in far_first(shards):
                to = lax.rem(dp + q, shards)
                from_here, to_there = d3_out[h].at[i, to], d3_in[h].at[i, dp]
                rcopy(from_here, to_there, dec_send.at[3 + h, i], half_recv.at[2, i, h], (sect, me, to)).start()
            d3_in[h][i, dp] = d3_out[h][i, dp]

        def give_back(h):
            first, size = firsts[h], sizes[h]
            wait_here(d3_in[h].at[i, pl.ds(0, shards - 1)], half_recv.at[2, i, h])
            total = d3_in[h][i, 0].astype(f32)
            for q in range(1, shards):
                total += d3_in[h][i, q].astype(f32)
            total = total.astype(bf16)
            back = dot(give_d[h][0], total[:, :LANES]) + dot(give_d[h][1], total[:, LANES:])
            d4_out[i, first : first + size] = back.astype(bf16).reshape(size, 8, LANES)
            for k in sect_far_first + ([0] if hand_over else []):
                place = (k - low) % experts
                if first <= place < first + size:
                    to = lax.rem(me + experts - k, experts)
                    home, slot = (other, 2) if hand_over else (sect, i)
                    rcopy(
                        d4_out.at[i, place], d4_in.at[slot, me], dec_send.at[5, i], ends_recv.at[slot], (home, to, dp)
                    ).start()

        gather(1)
        gather(0)
        if meanwhile is not None:
            meanwhile()
        near_act = up_part(1)
        down_part(0, up_part(0))
        down_part(1, near_act)
        give_back(0)
        give_back(1)
        if not hand_over:
            d4_in[i, me] = d4_out[i, own_place]
            mix(i, experts - 1)

    def mix(i, blocks):
        lane_ids = iota((2 * dec_rows, experts * 8), 1)
        weight = jnp.where(lane_ids == tcol_ref[i, 0], gcol_ref[i, 0], 0.0)
        weight += jnp.where(lane_ids == tcol_ref[i, 1], gcol_ref[i, 1], 0.0)
        high = weight.astype(bf16)
        rest = weight - high.astype(f32)
        middle = rest.astype(bf16)
        lowest = (rest - middle.astype(f32)).astype(bf16)
        wait_here(d4_in.at[i, pl.ds(0, blocks)], ends_recv.at[i])
        returned = d4_in[i].reshape(experts * 8, LANES)
        states_ref[...] += dot(high, returned) + (dot(middle, returned) + dot(lowest, returned))

    def decode_sent(i, blocks):
        wait_sent(d1_out.at[i, pl.ds(0, experts - 1)], dec_send.at[0, i])
        for h in range(2):
            wait_sent(xg[h].at[i, pl.ds(0, shards - 1)], dec_send.at[1 + h, i])
            wait_sent(d3_out[h].at[i, pl.ds(0, shards - 1)], dec_send.at[3 + h, i])
        wait_sent(d4_out.at[i, pl.ds(0, blocks)], dec_send.at[5, i])

    @pl.when(sect == 0)
    def _():
        for i in range(2):
            tables(i, i)
        loads[0].wait()
        rows = rows_v[...].astype(f32)
        states_ref[...] = jnp.concatenate([rows[:, :LANES], rows[:, LANES:]], axis=0)
        loads[1].wait()
        loads[2].wait()
        greeted()
        rcopy(own_v, held, l1_sem.at[0], l1_sem.at[1], (other, me, dp)).start()
        loads[3].wait()
        loads[4].wait()
        decode_step(0, up_v, down_v)
        rcopy(states_ref, states_ref, st_sem.at[0], st_sem.at[1], (other, me, dp)).start()
        decode_step(1, up_v, down_v, hand_over=True)
        wait_sent(states_ref, st_sem.at[0])
        wait_sent(held, l1_sem.at[0])
        decode_sent(0, experts - 1)
        decode_sent(1, experts)
        wait_here(fresh_up_ref, fresh_sem.at[0, 1])
        for i in range(2):
            wait_here(fresh_down_ref.at[pl.ds(i * (hidden // 2), hidden // 2)], fresh_sem.at[1 + i, 1])
        wait_here(final_ref, fin_sem.at[1])

    @pl.when(sect == 1)
    def _():
        lengths = len_ref[...].astype(f32)
        count = lengths.shape[1]
        length = jnp.concatenate([to_col(lengths[0:1]), to_col(lengths[1:2])], axis=0)
        both = 2 * count
        a, b = iota((both, both), 0), iota((both, both), 1)
        same_half = (a < count) == (b < count)
        start_row = jnp.sum(jnp.where(same_half & (a < b), length, 0.0), axis=0, keepdims=True)
        length_row = to_row(length)
        half_rows = held.shape[1]
        r, t = iota((2 * half_rows, both), 0), iota((2 * half_rows, both), 1)
        second = r >= half_rows
        row_in = r - jnp.where(second, float(half_rows), 0.0)
        offset = row_in - start_row
        inside = (second == (t >= count)) & (offset >= 0.0) & (offset < length_row)
        shard = pack_ref[...].astype(f32)
        target2 = jnp.sum(jnp.where(inside, shard * 8.0 + offset, 0.0), axis=1, keepdims=True)
        target2 = to_row(jnp.concatenate([target2, target2 + 4.0], axis=0))
        row_ids = iota((experts * 8, 4 * half_rows), 0)
        pack = ones_where(row_ids == target2)
        for load in loads:
            load.wait()
        for i in range(2):
            tables(i, i + 2)
        tables(2, 1)
        greeted()
        wait_here(held, l1_sem.at[1])
        for j in range(2):
            far, own = held[j], own_v[j]
            stacked = jnp.concatenate([far[:, :LANES], own[:, :LANES], far[:, LANES:], own[:, LANES:]], axis=0)
            out2[j] = dot(pack, stacked).astype(bf16).reshape(experts, 8, LANES)
            recv2[j, me] = out2[j, me]

        for k in sect_far_first:
            to = lax.rem(me + k, experts)
            rcopy(out2.at[:, to], recv2.at[:, me], l2_sem.at[0], l2_sem.at[1], (sect, to, dp)).start()

        lroutes = lroutes_ref[...].astype(f32)
        first, second = to_col(lroutes[0:1]), to_col(lroutes[1:2])
        within = ranks(first, second)
        gates = [to_col(lgates_ref[k : k + 1, :]) for k in range(2)]

        def by_half(col, step):
            n = col.shape[0]
            row = jnp.zeros((1, 2 * n), f32)
            r, l = iota((n, 2 * n), 0), iota((n, 2 * n), 1)
            source = jnp.floor(r * 0.25)
            place = source * 4.0 + r
            row += jnp.sum(jnp.where(l == place, col, 0.0), axis=0, keepdims=True)
            row += jnp.sum(jnp.where(l == place + 4.0, col + step, 0.0), axis=0, keepdims=True)
            return row

        stride = 2.0 * cap_l
        tr0 = by_half(first * stride + within[0], float(cap_l))
        tr1 = by_half(second * stride + within[1], float(cap_l))
        gr0, gr1 = by_half(gates[0], 0.0), by_half(gates[1], 0.0)
        ids = iota((experts * 2 * cap_l, experts * 8), 0)
        hit0, hit1 = ids == tr0, ids == tr1
        pick = ones_where(hit0 | hit1)
        scale = jnp.where(hit0, gr0, 0.0) + jnp.where(hit1, gr1, 0.0)
        high = scale.astype(bf16)
        low = (scale - high.astype(f32)).astype(bf16)
        wait_here(recv2.at[:, pl.ds(0, experts - 1)], l2_sem.at[1])
        inputs = recv2[0].reshape(experts * 8, LANES)
        cots = recv2[1].reshape(experts * 8, LANES)
        out3[0] = dot(pick, inputs).astype(bf16).reshape(experts, 2 * cap_l, LANES)
        out3[1] = (dot(high, cots) + dot(low, cots)).astype(bf16).reshape(experts, 2 * cap_l, LANES)
        for g in range(GROUPS):
            for k in sect_far_first:
                if k % GROUPS == g:
                    to = lax.rem(me + k, experts)
                    place = g * per + k // GROUPS
                    rcopy(out3.at[:, to], recv3.at[:, place], l3_send, l3_recv.at[g], (sect, to, dp)).start()
        recv3[0, 0] = out3[0, me]
        recv3[1, 0] = out3[1, me]

        nx = shards // 2
        right, left = lax.rem(ring + 1, nx), lax.rem(ring + nx - 1, nx)

        def at_ring(position):
            return (sect, me, position * 2 + core)

        def spread(g):
            first_in = 1 if g == 0 else 0
            if per - first_in:
                wait_here(recv3.at[:, pl.ds(g * per + first_in, per - first_in)], l3_recv.at[g])
            for j in range(2):
                rows = recv3[j, g * per : (g + 1) * per].reshape(per * 2 * cap_l, LANES)
                block = [dot(take_l[c], rows).astype(bf16) for c in range(2)]
                xg4[g, core, ring, j] = jnp.concatenate(block, axis=1)
            mine = xg4.at[g, core, ring]
            rcopy(mine, mine, l4_send.at[0, g], l4_recv.at[0, g], at_ring(right)).start()
            rcopy(mine, mine, l4_send.at[1, g], l4_recv.at[1, g], at_ring(left)).start()

        def relay(g):
            from_left, from_right = xg4.at[g, core, left], xg4.at[g, core, right]
            wait_here(from_left, l4_recv.at[0, g])
            on = from_left.at[0]
            rcopy(on, on, l4_send.at[2, g], l4_recv.at[2, g], at_ring(right)).start()
            wait_here(from_right, l4_recv.at[1, g])
            on = from_right.at[1]
            rcopy(on, on, l4_send.at[3, g], l4_recv.at[3, g], at_ring(left)).start()

        def share(g):
            across = xg4.at[g, core, lax.rem(ring + 2, nx)]
            wait_here(across.at[0], l4_recv.at[2, g])
            wait_here(across.at[1], l4_recv.at[3, g])
            mine = xg4.at[g, core]
            rcopy(mine, mine, l4_send.at[4, g], l4_recv.at[4, g], (sect, me, ring * 2 + 1 - core)).start()

        def hidden_parts(g):
            wait_here(xg4.at[g, 1 - core], l4_recv.at[4, g])
            pre = jnp.zeros((group_slots, hidden), f32)
            grad = jnp.zeros((group_slots, hidden), f32)
            for q in range(shards):
                cols = slice(q * part, (q + 1) * part)
                pre += dot_nt(xg4[g, q % 2, q // 2, 0], up_v[:, cols])
                grad += dot_nt(xg4[g, q % 2, q // 2, 1], down_v[:, cols])
            pre = pre * model_scale
            grad = grad * hidden_scale
            sig = 1.0 / (1.0 + jnp.exp(-pre))
            act_ref[g] = (pre * sig).astype(bf16)
            pre_ref[g] = (grad * sig * (1.0 + pre * (1.0 - sig))).astype(bf16)

        stages = (spread, relay, share, hidden_parts)
        for n in range(GROUPS + len(stages) - 1):
            for stage, run in enumerate(stages):
                if 0 <= n - stage < GROUPS:
                    run(n - stage)

        act = jnp.concatenate([act_ref[g] for g in range(GROUPS)], axis=0)
        pre = jnp.concatenate([pre_ref[g] for g in range(GROUPS)], axis=0)
        for j, (lhs, old, new, scale) in enumerate(
            ((pre, up_v, fresh_up_ref, model_scale), (act, down_v, fresh_down_ref, hidden_scale))
        ):
            for q in range(shards):
                cols = slice(q * part, (q + 1) * part)
                rhs = jnp.concatenate([xg4[g, q % 2, q // 2, j] for g in range(GROUPS)], axis=0)
                grad = dot_tn(lhs, rhs) * scale
                new[:, cols] = (old[:, cols].astype(f32) - step_size * grad).astype(bf16)
            if j == 0:
                rcopy(new, new, fresh_sem.at[j, 0], fresh_sem.at[j, 1], (other, me, dp)).start()

        wait_here(states_ref, st_sem.at[1])
        mix(2, experts)
        for i in range(2):

            def send_fresh(i=i):
                rows = pl.ds(i * (hidden // 2), hidden // 2)
                piece = fresh_down_ref.at[rows]
                rcopy(piece, piece, fresh_sem.at[1 + i, 0], fresh_sem.at[1 + i, 1], (other, me, dp)).start()

            decode_step(i, fresh_up_ref, fresh_down_ref, meanwhile=send_fresh)

        last = states_ref[...].astype(bf16)
        fin_src[...] = jnp.concatenate([last[:dec_rows], last[dec_rows:]], axis=1)
        near = shards // 2
        out_cols = pl.ds(pl.multiple_of(lax.rem(dp, near) * part, part), part)

        @pl.when(dp < near)
        def _():
            def send_far(q, carry):
                to = lax.rem(dp + q, shards)
                rcopy(fin_src, final_ref.at[:, out_cols], fin_sem.at[0], fin_sem.at[1], (other, me, to)).start()
                return carry

            lax.fori_loop(0, shards, send_far, 0)
            wait_here(final_ref, fin_sem.at[1])
            for _ in range(2):
                wait_sent(final_ref, fin_sem.at[0])

        @pl.when(dp >= near)
        def _():
            final_ref[:, out_cols] = fin_src[...]

            def send_near(q, carry):
                to = lax.rem(dp + q, shards)
                rcopy(fin_src, final_ref.at[:, out_cols], fin_sem.at[0], fin_sem.at[1], (sect, me, to)).start()
                return carry

            lax.fori_loop(1, shards, send_near, 0)
            wait_here(final_ref.at[:, pl.ds(0, (near - 1) * part)], fin_sem.at[1])
            wait_sent(final_ref, fin_sem.at[0])
            wait_sent(final_ref.at[:, pl.ds(0, (near - 1) * part)], fin_sem.at[0])

        for i in range(2):
            decode_sent(i, experts - 1)
        wait_sent(out2.at[:, pl.ds(0, experts - 1)], l2_sem.at[0])
        wait_sent(out3.at[:, pl.ds(0, experts - 1)], l3_send)
        for g in range(GROUPS):
            wait_sent(xg4.at[g, core, ring], l4_send.at[0, g])
            wait_sent(xg4.at[g, core, ring], l4_send.at[1, g])
            wait_sent(xg4.at[g, core, ring, 0], l4_send.at[2, g])
            wait_sent(xg4.at[g, core, ring, 1], l4_send.at[3, g])
            wait_sent(xg4.at[g, core], l4_send.at[4, g])
        wait_sent(fresh_up_ref, fresh_sem.at[0, 0])
        for i in range(2):
            wait_sent(fresh_down_ref.at[pl.ds(i * (hidden // 2), hidden // 2)], fresh_sem.at[1 + i, 0])


def on_device(
    decode_states, norm_gain, decode_routes, decode_gates, up_weight, down_weight,
    traj_inputs, traj_cotangents, traj_lengths, packing, learner_routes, learner_gates,
):
    experts, shards = lax.axis_size("exp"), lax.axis_size("dp")
    dec_rows, width = decode_states.shape
    lrn_rows = learner_routes.shape[0]
    part = width // shards
    hidden = up_weight.shape[2]
    cap_d = 3 * dec_rows * 2 // (2 * experts)
    cap_l = 3 * lrn_rows * 2 // (2 * experts)
    sizes = (experts // 4, experts - experts // 4)
    group_slots = experts // GROUPS * cap_l
    half_rows = traj_inputs.shape[1]
    vmem = pl.BlockSpec(memory_space=pltpu.VMEM)
    hbm = pl.BlockSpec(memory_space=pltpu.HBM)
    dma = pltpu.SemaphoreType.DMA
    final, fresh_up, fresh_down = pl.pallas_call(
        functools.partial(kernel, experts, shards, cap_d, cap_l),
        out_shape=(
            jax.ShapeDtypeStruct((dec_rows, width // 2), bf16),
            jax.ShapeDtypeStruct((hidden, width), bf16),
            jax.ShapeDtypeStruct((hidden, width), bf16),
        ),
        in_specs=[hbm, vmem, vmem, vmem, hbm, hbm, hbm, hbm, vmem, vmem, vmem, vmem],
        out_specs=(vmem,) * 3,
        scratch_shapes=[
            pltpu.VMEM((2, experts, 8, LANES), bf16),
            pltpu.VMEM((2, experts, 8, LANES), bf16),
            *[pltpu.VMEM((2, shards, size * cap_d, part), bf16) for _ in range(3) for size in sizes],
            pltpu.VMEM((2, experts, 8, LANES), bf16),
            pltpu.VMEM((3, experts, 8, LANES), bf16),
            pltpu.VMEM((2 * dec_rows, LANES), f32),
            pltpu.VMEM((3, 2, 1, 2 * dec_rows), f32),
            pltpu.VMEM((3, 2, 2 * dec_rows, 1), f32),
            pltpu.VMEM((3, 2, 2 * dec_rows, 1), f32),
            pltpu.VMEM((2, half_rows, part), bf16),
            pltpu.VMEM((2, experts, 8, LANES), bf16),
            pltpu.VMEM((2, experts, 8, LANES), bf16),
            pltpu.VMEM((2, experts, 2 * cap_l, LANES), bf16),
            pltpu.VMEM((2, experts, 2 * cap_l, LANES), bf16),
            pltpu.VMEM((GROUPS, 2, shards // 2, 2, group_slots, part), bf16),
            pltpu.VMEM((GROUPS, group_slots, hidden), bf16),
            pltpu.VMEM((GROUPS, group_slots, hidden), bf16),
            pltpu.VMEM((dec_rows, part), bf16),
            pltpu.VMEM((hidden, width), bf16),
            pltpu.VMEM((hidden, width), bf16),
            pltpu.VMEM((dec_rows, part), bf16),
            pltpu.VMEM((2, half_rows, part), bf16),
            *[pltpu.VMEM((2, size * cap_d, size * 8), bf16) for size in sizes],
            *[pltpu.VMEM((2, size * 8, size * cap_d), bf16) for size in sizes],
            pltpu.VMEM((2, group_slots, 2 * group_slots), bf16),
            dma((5,)),
            dma((6, 2)),
            dma((3,)),
            dma((3, 2, 2)),
            dma((2,)),
            dma((2,)),
            dma((2,)),
            dma((2,)),
            dma((3, 2)),
            dma,
            dma((GROUPS,)),
            dma((5, GROUPS)),
            dma((5, GROUPS)),
        ],
        compiler_params=pltpu.CompilerParams(
            collective_id=0, has_side_effects=True, vmem_limit_bytes=56 * 2**20
        ),
    )(
        decode_states, norm_gain.reshape(width // LANES, LANES),
        decode_routes.transpose(0, 2, 1), decode_gates.transpose(0, 2, 1),
        up_weight[0, 0], down_weight[0, 0], traj_inputs[0], traj_cotangents[0], traj_lengths[0], packing,
        learner_routes.T, learner_gates.T,
    )
    return final, fresh_up[None, None], fresh_down[None, None]


def solution(mesh):
    in_specs = (
        P("exp", None),
        P(),
        P(None, "exp", None),
        P(None, "exp", None),
        P("sect", "exp", "dp", None),
        P("sect", "exp", "dp", None),
        P("sect", "exp", None),
        P("sect", "exp", None),
        P("exp", None, None),
        P("exp", None),
        P("exp", None),
        P("exp", None),
    )
    out_specs = (P("exp", "sect"), P("sect", "exp", "dp", None), P("sect", "exp", "dp", None))
    return jax.shard_map(on_device, mesh=mesh, in_specs=in_specs, out_specs=out_specs, check_vma=False)
```

```python
import functools

import jax
import jax.numpy as jnp
from jax import lax
from jax.experimental import pallas as pl
from jax.experimental.pallas import tpu as pltpu
from jax.sharding import PartitionSpec as P

MESH = pl.DeviceIdType.MESH
step_size = 3.0
norm_eps = 1e-06
f32 = jnp.float32
bf16 = jnp.bfloat16
LANES = 128
GROUPS = 4


def dot(a, b):
    return lax.dot_general(a, b, (((1,), (0,)), ((), ())), preferred_element_type=f32)


def dot_nt(a, b):
    return lax.dot_general(a, b, (((1,), (1,)), ((), ())), preferred_element_type=f32)


def dot_tn(a, b):
    return lax.dot_general(a, b, (((0,), (0,)), ((), ())), preferred_element_type=f32)


def iota(shape, dim):
    return lax.broadcasted_iota(jnp.int32, shape, dim).astype(f32)


def to_row(col):
    n = col.shape[0]
    eye = iota((n, n), 0) == iota((n, n), 1)
    return jnp.sum(jnp.where(eye, col, 0.0), axis=0, keepdims=True)


def to_col(row):
    n = row.shape[1]
    eye = iota((n, n), 0) == iota((n, n), 1)
    return jnp.sum(jnp.where(eye, row, 0.0), axis=1, keepdims=True)


def ranks(first, second):
    n = first.shape[0]
    first_row, second_row = to_row(first), to_row(second)
    before = iota((n, n), 1) < iota((n, n), 0)
    out = []
    for mine in (first, second):
        same = ((first_row == mine) | (second_row == mine)) & before
        out.append(jnp.sum(jnp.where(same, 1.0, 0.0), axis=1, keepdims=True))
    return out


def far_first(count):
    return sorted(range(1, count), key=lambda k: (-min(k, count - k), k))


def slot_place(slot, per_source, block, c, half_step):
    source = jnp.floor((slot + 0.5) * (1.0 / per_source))
    return source * block + c * half_step + (slot - source * per_source)


def ones_where(condition):
    return jnp.where(condition, 1.0, 0.0).astype(bf16)


def kernel(
    experts, shards, cap_d, cap_l,
    rows_ref, gain_ref, routes_ref, gates_ref, up_ref, down_ref, in_ref, cot_ref, len_ref, pack_ref,
    lroutes_ref, lgates_ref,
    final_ref, fresh_up_ref, fresh_down_ref,
    d1_out, d1_in, xg_far, xg_near, d3_out_far, d3_out_near, d3_in_far, d3_in_near, d4_out, d4_in, states_ref, trow_ref, tcol_ref, gcol_ref,
    held, out2, recv2, out3, recv3, xg4, act_ref, pre_ref, fin_src,
    up_v, down_v, rows_v, own_v, take_far, take_near, give_far, give_near, take_l,
    load_sem, dec_send, ends_recv, half_recv, l1_sem, l2_sem, st_sem, fin_sem, fresh_sem, l3_send, l3_recv, l4_send, l4_recv,
):
    sect, me, dp = lax.axis_index("sect"), lax.axis_index("exp"), lax.axis_index("dp")
    ring, core = lax.div(dp, 2), lax.rem(dp, 2)
    other = 1 - sect
    width = rows_ref.shape[1]
    part = width // shards
    hidden = up_ref.shape[0]
    model_scale = width ** (-0.5)
    hidden_scale = (hidden * shards) ** (-0.5)
    dec_rows = rows_ref.shape[0]
    per = experts // GROUPS
    group_slots = per * cap_l
    col0 = pl.multiple_of(dp * part, part)
    sizes = (experts * 1 // 2, experts - experts * 1 // 2)
    firsts = (0, sizes[0])
    low = (experts - sizes[0] + 1) // 2
    xg, d3_out, d3_in = (xg_far, xg_near), (d3_out_far, d3_out_near), (d3_in_far, d3_in_near)
    take_d, give_d = (take_far, take_near), (give_far, give_near)
    sect_far_first = far_first(experts)
    loads = [
        pltpu.make_async_copy(rows_ref.at[:, pl.ds(col0, part)], rows_v, load_sem.at[0]),
        pltpu.make_async_copy(in_ref.at[:, pl.ds(col0, part)], own_v.at[0], load_sem.at[1]),
        pltpu.make_async_copy(cot_ref.at[:, pl.ds(col0, part)], own_v.at[1], load_sem.at[2]),
        pltpu.make_async_copy(up_ref, up_v, load_sem.at[3]),
        pltpu.make_async_copy(down_ref, down_v, load_sem.at[4]),
    ]

    def rcopy(src, dst, send, recv, device):
        return pltpu.make_async_remote_copy(
            src_ref=src, dst_ref=dst, send_sem=send, recv_sem=recv, device_id=device, device_id_type=MESH
        )

    def wait_sent(ref, sem):
        rcopy(ref, ref, sem, sem, (sect, me, dp)).wait_send()

    def wait_here(ref, sem):
        rcopy(ref, ref, sem, sem, (sect, me, dp)).wait_recv()

    barrier = pltpu.get_barrier_semaphore()

    for k in sect_far_first:
        pl.semaphore_signal(barrier, inc=1, device_id=(sect, lax.rem(me + k, experts), dp), device_id_type=MESH)
    for k in sect_far_first:
        pl.semaphore_signal(barrier, inc=1, device_id=(other, lax.rem(me + k, experts), dp), device_id_type=MESH)
    for q in range(1, shards):
        pl.semaphore_signal(barrier, inc=1, device_id=(sect, me, lax.rem(dp + q, shards)), device_id_type=MESH)
    for q in range(shards):
        pl.semaphore_signal(barrier, inc=1, device_id=(other, me, lax.rem(dp + q, shards)), device_id_type=MESH)
    for load in loads:
        load.start()
    for c in range(2):
        for h, size in enumerate(sizes):
            row, col = iota((size * cap_d, size * 8), 0), iota((size * cap_d, size * 8), 1)
            take_d[h][c] = ones_where(col == slot_place(row, cap_d, 8.0, c, 4.0))
            row, col = iota((size * 8, size * cap_d), 0), iota((size * 8, size * cap_d), 1)
            give_d[h][c] = ones_where(row == slot_place(col, cap_d, 8.0, c, 4.0))
        row, col = iota((group_slots, 2 * group_slots), 0), iota((group_slots, 2 * group_slots), 1)
        take_l[c] = ones_where(col == slot_place(row, cap_l, 2.0 * cap_l, c, float(cap_l)))

    def greeted():
        pl.semaphore_wait(barrier, 2 * (experts - 1) + shards - 1 + shards)

    def tables(i, t):
        routes = routes_ref[t].astype(f32)
        first, second = to_col(routes[0:1]), to_col(routes[1:2])
        within = ranks(first, second)
        for k, mine in enumerate((first, second)):
            target = mine * 8.0 + within[k]
            both = jnp.concatenate([target, target + 4.0], axis=0)
            tcol_ref[i, k] = both
            trow_ref[i, k] = to_row(both)
        for k in range(2):
            gate = to_col(gates_ref[t, k : k + 1, :])
            gcol_ref[i, k] = jnp.concatenate([gate, gate], axis=0)

    def decode_step(i, up, down, meanwhile=None, hand_over=False):
        gain0, gain1 = gain_ref[pl.ds(2 * dp, 1), :], gain_ref[pl.ds(2 * dp + 1, 1), :]
        gains = jnp.concatenate(
            [jnp.broadcast_to(gain0, (dec_rows, LANES)), jnp.broadcast_to(gain1, (dec_rows, LANES))], axis=0
        )
        y = (states_ref[...] * gains).astype(bf16)
        row_ids = iota((experts * 8, 2 * dec_rows), 0)
        pick = (row_ids == trow_ref[i, 0]) | (row_ids == trow_ref[i, 1])
        pick = jnp.where(pick, 1.0, 0.0).astype(bf16)
        d1_out[i] = dot(pick, y).astype(bf16).reshape(experts, 8, LANES)
        for k in sect_far_first:
            place = (k - low) % experts
            to = lax.rem(me + k, experts)
            arrival = half_recv.at[0, i, 0 if place < sizes[0] else 1]
            rcopy(d1_out.at[i, to], d1_in.at[i, place], dec_send.at[0, i], arrival, (sect, to, dp)).start()
        own_place = experts - low
        d1_in[i, own_place] = d1_out[i, me]

        def gather(h):
            first, size = firsts[h], sizes[h]
            wait_here(d1_in.at[i, pl.ds(first, size - h)], half_recv.at[0, i, h])
            arrived = d1_in[i, first : first + size].reshape(size * 8, LANES)
            block = [dot(take_d[h][c], arrived).astype(bf16) for c in range(2)]
            xg[h][i, dp] = jnp.concatenate(block, axis=1)
            mine = xg[h].at[i, dp]
            for q in far_first(shards):
                to = lax.rem(dp + q, shards)
                rcopy(mine, mine, dec_send.at[1 + h, i], half_recv.at[1, i, h], (sect, me, to)).start()

        def up_part(h):
            wait_here(xg[h].at[i, pl.ds(0, shards - 1)], half_recv.at[1, i, h])
            before_act = jnp.zeros((sizes[h] * cap_d, hidden), f32)
            squares = jnp.zeros((sizes[h] * cap_d, part), f32)
            for q in range(shards):
                piece = xg[h][i, q]
                before_act += dot_nt(piece, up[:, q * part : (q + 1) * part])
                gain = jnp.concatenate([gain_ref[2 * q : 2 * q + 1], gain_ref[2 * q + 1 : 2 * q + 2]], axis=1)
                wide = piece.astype(f32) * (1.0 / gain)
                squares += wide * wide
            mean = jnp.sum(squares, axis=1, keepdims=True) * (1.0 / width)
            before_act = before_act * (lax.rsqrt(mean + norm_eps) * model_scale)
            return (before_act / (1.0 + jnp.exp(-before_act))).astype(bf16)

        def down_part(h, act):
            for q in range(shards):
                d3_out[h][i, q] = (dot(act, down[:, q * part : (q + 1) * part]) * hidden_scale).astype(bf16)
            for q in far_first(shards):
                to = lax.rem(dp + q, shards)
                from_here, to_there = d3_out[h].at[i, to], d3_in[h].at[i, dp]
                rcopy(from_here, to_there, dec_send.at[3 + h, i], half_recv.at[2, i, h], (sect, me, to)).start()
            d3_in[h][i, dp] = d3_out[h][i, dp]

        def give_back(h):
            first, size = firsts[h], sizes[h]
            wait_here(d3_in[h].at[i, pl.ds(0, shards - 1)], half_recv.at[2, i, h])
            total = d3_in[h][i, 0].astype(f32)
            for q in range(1, shards):
                total += d3_in[h][i, q].astype(f32)
            total = total.astype(bf16)
            back = dot(give_d[h][0], total[:, :LANES]) + dot(give_d[h][1], total[:, LANES:])
            d4_out[i, first : first + size] = back.astype(bf16).reshape(size, 8, LANES)
            for k in sect_far_first + ([0] if hand_over else []):
                place = (k - low) % experts
                if first <= place < first + size:
                    to = lax.rem(me + experts - k, experts)
                    home, slot = (other, 2) if hand_over else (sect, i)
                    rcopy(
                        d4_out.at[i, place], d4_in.at[slot, me], dec_send.at[5, i], ends_recv.at[slot], (home, to, dp)
                    ).start()

        gather(1)
        gather(0)
        if meanwhile is not None:
            meanwhile()
        down_part(1, up_part(1))
        down_part(0, up_part(0))
        give_back(1)
        give_back(0)
        if not hand_over:
            d4_in[i, me] = d4_out[i, own_place]
            mix(i, experts - 1)

    def mix(i, blocks):
        lane_ids = iota((2 * dec_rows, experts * 8), 1)
        weight = jnp.where(lane_ids == tcol_ref[i, 0], gcol_ref[i, 0], 0.0)
        weight += jnp.where(lane_ids == tcol_ref[i, 1], gcol_ref[i, 1], 0.0)
        high = weight.astype(bf16)
        rest = weight - high.astype(f32)
        middle = rest.astype(bf16)
        lowest = (rest - middle.astype(f32)).astype(bf16)
        wait_here(d4_in.at[i, pl.ds(0, blocks)], ends_recv.at[i])
        returned = d4_in[i].reshape(experts * 8, LANES)
        states_ref[...] += dot(high, returned) + (dot(middle, returned) + dot(lowest, returned))

    def decode_sent(i, blocks):
        wait_sent(d1_out.at[i, pl.ds(0, experts - 1)], dec_send.at[0, i])
        for h in range(2):
            wait_sent(xg[h].at[i, pl.ds(0, shards - 1)], dec_send.at[1 + h, i])
            wait_sent(d3_out[h].at[i, pl.ds(0, shards - 1)], dec_send.at[3 + h, i])
        wait_sent(d4_out.at[i, pl.ds(0, blocks)], dec_send.at[5, i])

    @pl.when(sect == 0)
    def _():
        for i in range(2):
            tables(i, i)
        loads[0].wait()
        rows = rows_v[...].astype(f32)
        states_ref[...] = jnp.concatenate([rows[:, :LANES], rows[:, LANES:]], axis=0)
        loads[1].wait()
        loads[2].wait()
        greeted()
        rcopy(own_v, held, l1_sem.at[0], l1_sem.at[1], (other, me, dp)).start()
        loads[3].wait()
        loads[4].wait()
        decode_step(0, up_v, down_v)
        rcopy(states_ref, states_ref, st_sem.at[0], st_sem.at[1], (other, me, dp)).start()
        decode_step(1, up_v, down_v, hand_over=True)
        wait_sent(states_ref, st_sem.at[0])
        wait_sent(held, l1_sem.at[0])
        decode_sent(0, experts - 1)
        decode_sent(1, experts)
        wait_here(fresh_up_ref, fresh_sem.at[0, 1])
        for i in range(2):
            wait_here(fresh_down_ref.at[pl.ds(i * (hidden // 2), hidden // 2)], fresh_sem.at[1 + i, 1])
        wait_here(final_ref, fin_sem.at[1])

    @pl.when(sect == 1)
    def _():
        lengths = len_ref[...].astype(f32)
        count = lengths.shape[1]
        length = jnp.concatenate([to_col(lengths[0:1]), to_col(lengths[1:2])], axis=0)
        both = 2 * count
        a, b = iota((both, both), 0), iota((both, both), 1)
        same_half = (a < count) == (b < count)
        start_row = jnp.sum(jnp.where(same_half & (a < b), length, 0.0), axis=0, keepdims=True)
        length_row = to_row(length)
        half_rows = held.shape[1]
        r, t = iota((2 * half_rows, both), 0), iota((2 * half_rows, both), 1)
        second = r >= half_rows
        row_in = r - jnp.where(second, float(half_rows), 0.0)
        offset = row_in - start_row
        inside = (second == (t >= count)) & (offset >= 0.0) & (offset < length_row)
        shard = pack_ref[...].astype(f32)
        target2 = jnp.sum(jnp.where(inside, shard * 8.0 + offset, 0.0), axis=1, keepdims=True)
        target2 = to_row(jnp.concatenate([target2, target2 + 4.0], axis=0))
        row_ids = iota((experts * 8, 4 * half_rows), 0)
        pack = ones_where(row_ids == target2)
        for load in loads:
            load.wait()
        for i in range(2):
            tables(i, i + 2)
        tables(2, 1)
        greeted()
        wait_here(held, l1_sem.at[1])
        for j in range(2):
            far, own = held[j], own_v[j]
            stacked = jnp.concatenate([far[:, :LANES], own[:, :LANES], far[:, LANES:], own[:, LANES:]], axis=0)
            out2[j] = dot(pack, stacked).astype(bf16).reshape(experts, 8, LANES)
            recv2[j, me] = out2[j, me]

        for k in sect_far_first:
            to = lax.rem(me + k, experts)
            rcopy(out2.at[:, to], recv2.at[:, me], l2_sem.at[0], l2_sem.at[1], (sect, to, dp)).start()

        lroutes = lroutes_ref[...].astype(f32)
        first, second = to_col(lroutes[0:1]), to_col(lroutes[1:2])
        within = ranks(first, second)
        gates = [to_col(lgates_ref[k : k + 1, :]) for k in range(2)]

        def by_half(col, step):
            n = col.shape[0]
            row = jnp.zeros((1, 2 * n), f32)
            r, l = iota((n, 2 * n), 0), iota((n, 2 * n), 1)
            source = jnp.floor(r * 0.25)
            place = source * 4.0 + r
            row += jnp.sum(jnp.where(l == place, col, 0.0), axis=0, keepdims=True)
            row += jnp.sum(jnp.where(l == place + 4.0, col + step, 0.0), axis=0, keepdims=True)
            return row

        stride = 2.0 * cap_l
        tr0 = by_half(first * stride + within[0], float(cap_l))
        tr1 = by_half(second * stride + within[1], float(cap_l))
        gr0, gr1 = by_half(gates[0], 0.0), by_half(gates[1], 0.0)
        ids = iota((experts * 2 * cap_l, experts * 8), 0)
        hit0, hit1 = ids == tr0, ids == tr1
        pick = ones_where(hit0 | hit1)
        scale = jnp.where(hit0, gr0, 0.0) + jnp.where(hit1, gr1, 0.0)
        high = scale.astype(bf16)
        low = (scale - high.astype(f32)).astype(bf16)
        wait_here(recv2.at[:, pl.ds(0, experts - 1)], l2_sem.at[1])
        inputs = recv2[0].reshape(experts * 8, LANES)
        cots = recv2[1].reshape(experts * 8, LANES)
        out3[0] = dot(pick, inputs).astype(bf16).reshape(experts, 2 * cap_l, LANES)
        out3[1] = (dot(high, cots) + dot(low, cots)).astype(bf16).reshape(experts, 2 * cap_l, LANES)
        for g in range(GROUPS):
            for k in sect_far_first:
                if k % GROUPS == g:
                    to = lax.rem(me + k, experts)
                    place = g * per + k // GROUPS
                    rcopy(out3.at[:, to], recv3.at[:, place], l3_send, l3_recv.at[g], (sect, to, dp)).start()
        recv3[0, 0] = out3[0, me]
        recv3[1, 0] = out3[1, me]

        nx = shards // 2
        right, left = lax.rem(ring + 1, nx), lax.rem(ring + nx - 1, nx)

        def at_ring(position):
            return (sect, me, position * 2 + core)

        def spread(g):
            first_in = 1 if g == 0 else 0
            if per - first_in:
                wait_here(recv3.at[:, pl.ds(g * per + first_in, per - first_in)], l3_recv.at[g])
            for j in range(2):
                rows = recv3[j, g * per : (g + 1) * per].reshape(per * 2 * cap_l, LANES)
                block = [dot(take_l[c], rows).astype(bf16) for c in range(2)]
                xg4[g, core, ring, j] = jnp.concatenate(block, axis=1)
            mine = xg4.at[g, core, ring]
            rcopy(mine, mine, l4_send.at[0, g], l4_recv.at[0, g], at_ring(right)).start()
            rcopy(mine, mine, l4_send.at[1, g], l4_recv.at[1, g], at_ring(left)).start()

        def relay(g):
            from_left, from_right = xg4.at[g, core, left], xg4.at[g, core, right]
            wait_here(from_left, l4_recv.at[0, g])
            on = from_left.at[0]
            rcopy(on, on, l4_send.at[2, g], l4_recv.at[2, g], at_ring(right)).start()
            wait_here(from_right, l4_recv.at[1, g])
            on = from_right.at[1]
            rcopy(on, on, l4_send.at[3, g], l4_recv.at[3, g], at_ring(left)).start()

        def share(g):
            across = xg4.at[g, core, lax.rem(ring + 2, nx)]
            wait_here(across.at[0], l4_recv.at[2, g])
            wait_here(across.at[1], l4_recv.at[3, g])
            mine = xg4.at[g, core]
            rcopy(mine, mine, l4_send.at[4, g], l4_recv.at[4, g], (sect, me, ring * 2 + 1 - core)).start()

        def hidden_parts(g):
            wait_here(xg4.at[g, 1 - core], l4_recv.at[4, g])
            pre = jnp.zeros((group_slots, hidden), f32)
            grad = jnp.zeros((group_slots, hidden), f32)
            for q in range(shards):
                cols = slice(q * part, (q + 1) * part)
                pre += dot_nt(xg4[g, q % 2, q // 2, 0], up_v[:, cols])
                grad += dot_nt(xg4[g, q % 2, q // 2, 1], down_v[:, cols])
            pre = pre * model_scale
            grad = grad * hidden_scale
            sig = 1.0 / (1.0 + jnp.exp(-pre))
            act_ref[g] = (pre * sig).astype(bf16)
            pre_ref[g] = (grad * sig * (1.0 + pre * (1.0 - sig))).astype(bf16)

        stages = (spread, relay, share, hidden_parts)
        for n in range(GROUPS + len(stages) - 1):
            for stage, run in enumerate(stages):
                if 0 <= n - stage < GROUPS:
                    run(n - stage)

        act = jnp.concatenate([act_ref[g] for g in range(GROUPS)], axis=0)
        pre = jnp.concatenate([pre_ref[g] for g in range(GROUPS)], axis=0)
        for j, (lhs, old, new, scale) in enumerate(
            ((pre, up_v, fresh_up_ref, model_scale), (act, down_v, fresh_down_ref, hidden_scale))
        ):
            for q in range(shards):
                cols = slice(q * part, (q + 1) * part)
                rhs = jnp.concatenate([xg4[g, q % 2, q // 2, j] for g in range(GROUPS)], axis=0)
                grad = dot_tn(lhs, rhs) * scale
                new[:, cols] = (old[:, cols].astype(f32) - step_size * grad).astype(bf16)
            if j == 0:
                rcopy(new, new, fresh_sem.at[j, 0], fresh_sem.at[j, 1], (other, me, dp)).start()

        wait_here(states_ref, st_sem.at[1])
        mix(2, experts)
        for i in range(2):

            def send_fresh(i=i):
                rows = pl.ds(i * (hidden // 2), hidden // 2)
                piece = fresh_down_ref.at[rows]
                rcopy(piece, piece, fresh_sem.at[1 + i, 0], fresh_sem.at[1 + i, 1], (other, me, dp)).start()

            decode_step(i, fresh_up_ref, fresh_down_ref, meanwhile=send_fresh)

        last = states_ref[...].astype(bf16)
        fin_src[...] = jnp.concatenate([last[:dec_rows], last[dec_rows:]], axis=1)
        near = shards // 2
        out_cols = pl.ds(pl.multiple_of(lax.rem(dp, near) * part, part), part)

        @pl.when(dp < near)
        def _():
            def send_far(q, carry):
                to = lax.rem(dp + q, shards)
                rcopy(fin_src, final_ref.at[:, out_cols], fin_sem.at[0], fin_sem.at[1], (other, me, to)).start()
                return carry

            lax.fori_loop(0, shards, send_far, 0)
            wait_here(final_ref, fin_sem.at[1])
            for _ in range(2):
                wait_sent(final_ref, fin_sem.at[0])

        @pl.when(dp >= near)
        def _():
            final_ref[:, out_cols] = fin_src[...]

            def send_near(q, carry):
                to = lax.rem(dp + q, shards)
                rcopy(fin_src, final_ref.at[:, out_cols], fin_sem.at[0], fin_sem.at[1], (sect, me, to)).start()
                return carry

            lax.fori_loop(1, shards, send_near, 0)
            wait_here(final_ref.at[:, pl.ds(0, (near - 1) * part)], fin_sem.at[1])
            wait_sent(final_ref, fin_sem.at[0])
            wait_sent(final_ref.at[:, pl.ds(0, (near - 1) * part)], fin_sem.at[0])

        for i in range(2):
            decode_sent(i, experts - 1)
        wait_sent(out2.at[:, pl.ds(0, experts - 1)], l2_sem.at[0])
        wait_sent(out3.at[:, pl.ds(0, experts - 1)], l3_send)
        for g in range(GROUPS):
            wait_sent(xg4.at[g, core, ring], l4_send.at[0, g])
            wait_sent(xg4.at[g, core, ring], l4_send.at[1, g])
            wait_sent(xg4.at[g, core, ring, 0], l4_send.at[2, g])
            wait_sent(xg4.at[g, core, ring, 1], l4_send.at[3, g])
            wait_sent(xg4.at[g, core], l4_send.at[4, g])
        wait_sent(fresh_up_ref, fresh_sem.at[0, 0])
        for i in range(2):
            wait_sent(fresh_down_ref.at[pl.ds(i * (hidden // 2), hidden // 2)], fresh_sem.at[1 + i, 0])


def on_device(
    decode_states, norm_gain, decode_routes, decode_gates, up_weight, down_weight,
    traj_inputs, traj_cotangents, traj_lengths, packing, learner_routes, learner_gates,
):
    experts, shards = lax.axis_size("exp"), lax.axis_size("dp")
    dec_rows, width = decode_states.shape
    lrn_rows = learner_routes.shape[0]
    part = width // shards
    hidden = up_weight.shape[2]
    cap_d = 3 * dec_rows * 2 // (2 * experts)
    cap_l = 3 * lrn_rows * 2 // (2 * experts)
    sizes = (experts * 1 // 2, experts - experts * 1 // 2)
    group_slots = experts // GROUPS * cap_l
    half_rows = traj_inputs.shape[1]
    vmem = pl.BlockSpec(memory_space=pltpu.VMEM)
    hbm = pl.BlockSpec(memory_space=pltpu.HBM)
    dma = pltpu.SemaphoreType.DMA
    keep = functools.partial(pltpu.with_memory_space_constraint, memory_space=pltpu.HBM)
    final, fresh_up, fresh_down = pl.pallas_call(
        functools.partial(kernel, experts, shards, cap_d, cap_l),
        out_shape=(
            jax.ShapeDtypeStruct((dec_rows, width // 2), bf16),
            jax.ShapeDtypeStruct((hidden, width), bf16),
            jax.ShapeDtypeStruct((hidden, width), bf16),
        ),
        in_specs=[hbm, vmem, vmem, vmem, hbm, hbm, hbm, hbm, vmem, vmem, vmem, vmem],
        out_specs=(vmem,) * 3,
        scratch_shapes=[
            pltpu.VMEM((2, experts, 8, LANES), bf16),
            pltpu.VMEM((2, experts, 8, LANES), bf16),
            *[pltpu.VMEM((2, shards, size * cap_d, part), bf16) for _ in range(3) for size in sizes],
            pltpu.VMEM((2, experts, 8, LANES), bf16),
            pltpu.VMEM((3, experts, 8, LANES), bf16),
            pltpu.VMEM((2 * dec_rows, LANES), f32),
            pltpu.VMEM((3, 2, 1, 2 * dec_rows), f32),
            pltpu.VMEM((3, 2, 2 * dec_rows, 1), f32),
            pltpu.VMEM((3, 2, 2 * dec_rows, 1), f32),
            pltpu.VMEM((2, half_rows, part), bf16),
            pltpu.VMEM((2, experts, 8, LANES), bf16),
            pltpu.VMEM((2, experts, 8, LANES), bf16),
            pltpu.VMEM((2, experts, 2 * cap_l, LANES), bf16),
            pltpu.VMEM((2, experts, 2 * cap_l, LANES), bf16),
            pltpu.VMEM((GROUPS, 2, shards // 2, 2, group_slots, part), bf16),
            pltpu.VMEM((GROUPS, group_slots, hidden), bf16),
            pltpu.VMEM((GROUPS, group_slots, hidden), bf16),
            pltpu.VMEM((dec_rows, part), bf16),
            pltpu.VMEM((hidden, width), bf16),
            pltpu.VMEM((hidden, width), bf16),
            pltpu.VMEM((dec_rows, part), bf16),
            pltpu.VMEM((2, half_rows, part), bf16),
            *[pltpu.VMEM((2, size * cap_d, size * 8), bf16) for size in sizes],
            *[pltpu.VMEM((2, size * 8, size * cap_d), bf16) for size in sizes],
            pltpu.VMEM((2, group_slots, 2 * group_slots), bf16),
            dma((5,)),
            dma((6, 2)),
            dma((3,)),
            dma((3, 2, 2)),
            dma((2,)),
            dma((2,)),
            dma((2,)),
            dma((2,)),
            dma((3, 2)),
            dma,
            dma((GROUPS,)),
            dma((5, GROUPS)),
            dma((5, GROUPS)),
        ],
        compiler_params=pltpu.CompilerParams(
            collective_id=0, has_side_effects=True, vmem_limit_bytes=40 * 2**20
        ),
    )(
        keep(decode_states), norm_gain.reshape(width // LANES, LANES),
        decode_routes.transpose(0, 2, 1), decode_gates.transpose(0, 2, 1),
        keep(up_weight[0, 0]), keep(down_weight[0, 0]), keep(traj_inputs[0]), keep(traj_cotangents[0]), traj_lengths[0], packing,
        learner_routes.T, learner_gates.T,
    )
    return final, fresh_up[None, None], fresh_down[None, None]


def solution(mesh):
    in_specs = (
        P("exp", None),
        P(),
        P(None, "exp", None),
        P(None, "exp", None),
        P("sect", "exp", "dp", None),
        P("sect", "exp", "dp", None),
        P("sect", "exp", None),
        P("sect", "exp", None),
        P("exp", None, None),
        P("exp", None),
        P("exp", None),
        P("exp", None),
    )
    out_specs = (P("exp", "sect"), P("sect", "exp", "dp", None), P("sect", "exp", "dp", None))
    return jax.shard_map(on_device, mesh=mesh, in_specs=in_specs, out_specs=out_specs, check_vma=False)
```

```python
import functools

import jax
import jax.numpy as jnp
from jax import lax
from jax.experimental import pallas as pl
from jax.experimental.pallas import tpu as pltpu
from jax.sharding import PartitionSpec as P

MESH = pl.DeviceIdType.MESH
step_size = 3.0
norm_eps = 1e-06
f32 = jnp.float32
bf16 = jnp.bfloat16
LANES = 128
GROUPS = 4


def dot(a, b):
    return lax.dot_general(a, b, (((1,), (0,)), ((), ())), preferred_element_type=f32)


def dot_nt(a, b):
    return lax.dot_general(a, b, (((1,), (1,)), ((), ())), preferred_element_type=f32)


def dot_tn(a, b):
    return lax.dot_general(a, b, (((0,), (0,)), ((), ())), preferred_element_type=f32)


def iota(shape, dim):
    return lax.broadcasted_iota(jnp.int32, shape, dim).astype(f32)


def to_row(col):
    n = col.shape[0]
    eye = iota((n, n), 0) == iota((n, n), 1)
    return jnp.sum(jnp.where(eye, col, 0.0), axis=0, keepdims=True)


def to_col(row):
    n = row.shape[1]
    eye = iota((n, n), 0) == iota((n, n), 1)
    return jnp.sum(jnp.where(eye, row, 0.0), axis=1, keepdims=True)


def ranks(first, second):
    n = first.shape[0]
    first_row, second_row = to_row(first), to_row(second)
    before = iota((n, n), 1) < iota((n, n), 0)
    out = []
    for mine in (first, second):
        same = ((first_row == mine) | (second_row == mine)) & before
        out.append(jnp.sum(jnp.where(same, 1.0, 0.0), axis=1, keepdims=True))
    return out


def far_first(count):
    return sorted(range(1, count), key=lambda k: (-min(k, count - k), k))


def slot_place(slot, per_source, block, c, half_step):
    source = jnp.floor((slot + 0.5) * (1.0 / per_source))
    return source * block + c * half_step + (slot - source * per_source)


def ones_where(condition):
    return jnp.where(condition, 1.0, 0.0).astype(bf16)


def kernel(
    experts, shards, cap_d, cap_l,
    rows_ref, gain_ref, routes_ref, gates_ref, up_ref, down_ref, in_ref, cot_ref, len_ref, pack_ref,
    lroutes_ref, lgates_ref,
    final_ref, fresh_up_ref, fresh_down_ref,
    d1_out, d1_in, xg_far, xg_near, d3_out_far, d3_out_near, d3_in_far, d3_in_near, pair_in, d3_sum, d4_out, d4_in, states_ref, last_ref, trow_ref, tcol_ref, gcol_ref,
    held, out2, recv2, out3, recv3, xg4, act_ref, pre_ref, fin_src,
    up_v, down_v, rows_v, own_v, take_far, take_near, give_far, give_near, take_l,
    load_sem, dec_send, ends_recv, half_recv, pair_recv, l1_sem, l2_sem, st_sem, last_sem, fin_sem, fresh_sem, l3_send, l3_recv, l4_send, l4_recv,
):
    sect, me, dp = lax.axis_index("sect"), lax.axis_index("exp"), lax.axis_index("dp")
    ring, core = lax.div(dp, 2), lax.rem(dp, 2)
    other = 1 - sect
    width = rows_ref.shape[1]
    part = width // shards
    hidden = up_ref.shape[0]
    model_scale = width ** (-0.5)
    hidden_scale = (hidden * shards) ** (-0.5)
    dec_rows = rows_ref.shape[0]
    per = experts // GROUPS
    group_slots = per * cap_l
    col0 = pl.multiple_of(dp * part, part)
    sizes = (experts * 3 // 8, experts - experts * 3 // 8)
    firsts = (0, sizes[0])
    low = (experts - sizes[0] + 1) // 2
    take_d, give_d = (take_far, take_near), (give_far, give_near)
    sect_far_first = far_first(experts)
    loads = [
        pltpu.make_async_copy(rows_ref.at[:, pl.ds(col0, part)], rows_v, load_sem.at[0]),
        pltpu.make_async_copy(in_ref.at[:, pl.ds(col0, part)], own_v.at[0], load_sem.at[1]),
        pltpu.make_async_copy(cot_ref.at[:, pl.ds(col0, part)], own_v.at[1], load_sem.at[2]),
        pltpu.make_async_copy(up_ref, up_v, load_sem.at[3]),
        pltpu.make_async_copy(down_ref, down_v, load_sem.at[4]),
    ]

    def rcopy(src, dst, send, recv, device):
        return pltpu.make_async_remote_copy(
            src_ref=src, dst_ref=dst, send_sem=send, recv_sem=recv, device_id=device, device_id_type=MESH
        )

    nx = shards // 2
    near_dp = shards // 2
    sibling = (sect, me, ring * 2 + 1 - core)

    def at_ring(position):
        return (sect, me, position * 2 + core)

    def wait_sent(ref, sem):
        rcopy(ref, ref, sem, sem, (sect, me, dp)).wait_send()

    def wait_here(ref, sem):
        rcopy(ref, ref, sem, sem, (sect, me, dp)).wait_recv()

    barrier = pltpu.get_barrier_semaphore()

    for k in sect_far_first:
        pl.semaphore_signal(barrier, inc=1, device_id=(sect, lax.rem(me + k, experts), dp), device_id_type=MESH)
    for k in sect_far_first:
        pl.semaphore_signal(barrier, inc=1, device_id=(other, lax.rem(me + k, experts), dp), device_id_type=MESH)
    for q in range(1, shards):
        pl.semaphore_signal(barrier, inc=1, device_id=(sect, me, lax.rem(dp + q, shards)), device_id_type=MESH)
    for q in range(shards):
        pl.semaphore_signal(barrier, inc=1, device_id=(other, me, lax.rem(dp + q, shards)), device_id_type=MESH)
    for load in loads:
        load.start()
    for c in range(2):
        for h, size in enumerate(sizes):
            row, col = iota((size * cap_d, size * 8), 0), iota((size * cap_d, size * 8), 1)
            take_d[h][c] = ones_where(col == slot_place(row, cap_d, 8.0, c, 4.0))
            row, col = iota((size * 8, size * cap_d), 0), iota((size * 8, size * cap_d), 1)
            give_d[h][c] = ones_where(row == slot_place(col, cap_d, 8.0, c, 4.0))
        row, col = iota((group_slots, 2 * group_slots), 0), iota((group_slots, 2 * group_slots), 1)
        take_l[c] = ones_where(col == slot_place(row, cap_l, 2.0 * cap_l, c, float(cap_l)))

    def greeted():
        pl.semaphore_wait(barrier, 2 * (experts - 1) + shards - 1 + shards)

    def tables(i, t):
        routes = routes_ref[t].astype(f32)
        first, second = to_col(routes[0:1]), to_col(routes[1:2])
        within = ranks(first, second)
        for k, mine in enumerate((first, second)):
            target = mine * 8.0 + within[k]
            both = jnp.concatenate([target, target + 4.0], axis=0)
            tcol_ref[i, k] = both
            trow_ref[i, k] = to_row(both)
        for k in range(2):
            gate = to_col(gates_ref[t, k : k + 1, :])
            gcol_ref[i, k] = jnp.concatenate([gate, gate], axis=0)

    def decode_step(i, up, down, meanwhile=None, hand_over=False, split=False):
        gain0, gain1 = gain_ref[pl.ds(2 * dp, 1), :], gain_ref[pl.ds(2 * dp + 1, 1), :]
        gains = jnp.concatenate(
            [jnp.broadcast_to(gain0, (dec_rows, LANES)), jnp.broadcast_to(gain1, (dec_rows, LANES))], axis=0
        )
        y = (states_ref[...] * gains).astype(bf16)
        row_ids = iota((experts * 8, 2 * dec_rows), 0)
        pick = (row_ids == trow_ref[i, 0]) | (row_ids == trow_ref[i, 1])
        pick = jnp.where(pick, 1.0, 0.0).astype(bf16)
        d1_out[i] = dot(pick, y).astype(bf16).reshape(experts, 8, LANES)
        for k in sect_far_first:
            place = (k - low) % experts
            to = lax.rem(me + k, experts)
            arrival = half_recv.at[0, i, 0 if place < sizes[0] else 1]
            rcopy(d1_out.at[i, to], d1_in.at[i, place], dec_send.at[0, i], arrival, (sect, to, dp)).start()
        own_place = experts - low
        d1_in[i, own_place] = d1_out[i, me]

        def gather(h):
            first, size = firsts[h], sizes[h]
            wait_here(d1_in.at[i, pl.ds(first, size - h)], half_recv.at[0, i, h])
            arrived = d1_in[i, first : first + size].reshape(size * 8, LANES)
            block = [dot(take_d[h][c], arrived).astype(bf16) for c in range(2)]
            if h == 0:
                xg_far[i, dp] = jnp.concatenate(block, axis=1)
                mine = xg_far.at[i, dp]
                for q in far_first(shards):
                    to = lax.rem(dp + q, shards)
                    rcopy(mine, mine, dec_send.at[1, i], half_recv.at[1, i, 0], (sect, me, to)).start()
            else:
                xg_near[i, core, ring] = jnp.concatenate(block, axis=1)
                mine = xg_near.at[i, core, ring]
                for k in far_first(nx):
                    to = at_ring(lax.rem(ring + k, nx))
                    rcopy(mine, mine, dec_send.at[2, i], half_recv.at[1, i, 1], to).start()

        def share_near():
            wait_here(xg_near.at[i, core, pl.ds(0, nx - 1)], half_recv.at[1, i, 1])
            mine = xg_near.at[i, core]
            rcopy(mine, mine, dec_send.at[6, i], pair_recv.at[0, i], sibling).start()

        def up_part(h):
            if h == 0:
                wait_here(xg_far.at[i, pl.ds(0, shards - 1)], half_recv.at[1, i, 0])
            else:
                wait_here(xg_near.at[i, 1 - core], pair_recv.at[0, i])
            before_act = jnp.zeros((sizes[h] * cap_d, hidden), f32)
            squares = jnp.zeros((sizes[h] * cap_d, part), f32)
            for q in range(shards):
                piece = xg_far[i, q] if h == 0 else xg_near[i, q % 2, q // 2]
                before_act += dot_nt(piece, up[:, q * part : (q + 1) * part])
                gain = jnp.concatenate([gain_ref[2 * q : 2 * q + 1], gain_ref[2 * q + 1 : 2 * q + 2]], axis=1)
                wide = piece.astype(f32) * (1.0 / gain)
                squares += wide * wide
            mean = jnp.sum(squares, axis=1, keepdims=True) * (1.0 / width)
            before_act = before_act * (lax.rsqrt(mean + norm_eps) * model_scale)
            return (before_act / (1.0 + jnp.exp(-before_act))).astype(bf16)

        def down_part(h, act):
            for q in range(shards):
                piece = (dot(act, down[:, q * part : (q + 1) * part]) * hidden_scale).astype(bf16)
                if h == 0:
                    d3_out_far[i, q] = piece
                else:
                    d3_out_near[i, q % 2, q // 2] = piece
            if h == 0:
                for q in far_first(shards):
                    to = lax.rem(dp + q, shards)
                    from_here, to_there = d3_out_far.at[i, to], d3_in_far.at[i, dp]
                    rcopy(from_here, to_there, dec_send.at[3, i], half_recv.at[2, i, 0], (sect, me, to)).start()
                d3_in_far[i, dp] = d3_out_far[i, dp]
            else:
                theirs = d3_out_near.at[i, 1 - core]
                rcopy(theirs, pair_in.at[i], dec_send.at[7, i], pair_recv.at[1, i], sibling).start()

        def scatter_near():
            wait_here(pair_in.at[i], pair_recv.at[1, i])
            d3_sum[i] = (d3_out_near[i, core].astype(f32) + pair_in[i].astype(f32)).astype(bf16)
            for k in far_first(nx):
                to = lax.rem(ring + k, nx)
                from_here, to_there = d3_sum.at[i, to], d3_in_near.at[i, ring]
                rcopy(from_here, to_there, dec_send.at[4, i], half_recv.at[2, i, 1], at_ring(to)).start()
            d3_in_near[i, ring] = d3_sum[i, ring]

        def give_back(h):
            first, size = firsts[h], sizes[h]
            d3_in, count = (d3_in_far, shards) if h == 0 else (d3_in_near, nx)
            wait_here(d3_in.at[i, pl.ds(0, count - 1)], half_recv.at[2, i, h])
            total = d3_in[i, 0].astype(f32)
            for q in range(1, count):
                total += d3_in[i, q].astype(f32)
            total = total.astype(bf16)
            back = dot(give_d[h][0], total[:, :LANES]) + dot(give_d[h][1], total[:, LANES:])
            d4_out[i, first : first + size] = back.astype(bf16).reshape(size, 8, LANES)
            for k in sect_far_first + ([0] if hand_over else []):
                place = (k - low) % experts
                if first <= place < first + size:
                    to = lax.rem(me + experts - k, experts)
                    home, slot = (other, 2) if hand_over else (sect, i)
                    if split:
                        home, slot = jnp.where(dp < near_dp, other, sect), jnp.where(dp < near_dp, 2, i)
                    rcopy(
                        d4_out.at[i, place], d4_in.at[slot, me], dec_send.at[5, i], ends_recv.at[slot], (home, to, dp)
                    ).start()

        gather(1)
        gather(0)
        share_near()
        if meanwhile is not None:
            meanwhile()
        near_act = up_part(1)
        down_part(0, up_part(0))
        down_part(1, near_act)
        scatter_near()
        give_back(0)
        give_back(1)
        if split:
            @pl.when(dp < near_dp)
            def _():
                rcopy(
                    d4_out.at[i, own_place], d4_in.at[2, me], dec_send.at[5, i], ends_recv.at[2], (other, me, dp)
                ).start()

            @pl.when(dp >= near_dp)
            def _():
                d4_in[i, me] = d4_out[i, own_place]
                mix(i, experts - 1, states_ref)
        elif not hand_over:
            d4_in[i, me] = d4_out[i, own_place]
            mix(i, experts - 1, states_ref)

    def mix(i, blocks, onto):
        lane_ids = iota((2 * dec_rows, experts * 8), 1)
        weight = jnp.where(lane_ids == tcol_ref[i, 0], gcol_ref[i, 0], 0.0)
        weight += jnp.where(lane_ids == tcol_ref[i, 1], gcol_ref[i, 1], 0.0)
        high = weight.astype(bf16)
        rest = weight - high.astype(f32)
        middle = rest.astype(bf16)
        lowest = (rest - middle.astype(f32)).astype(bf16)
        wait_here(d4_in.at[i, pl.ds(0, blocks)], ends_recv.at[i])
        returned = d4_in[i].reshape(experts * 8, LANES)
        onto[...] += dot(high, returned) + (dot(middle, returned) + dot(lowest, returned))

    out_cols = pl.ds(pl.multiple_of(lax.rem(dp, near_dp) * part, part), part)

    def finish(from_ref):
        last = from_ref[...].astype(bf16)
        fin_src[...] = jnp.concatenate([last[:dec_rows], last[dec_rows:]], axis=1)
        for q in far_first(shards):
            to = lax.rem(dp + q, shards)
            rcopy(fin_src, final_ref.at[:, out_cols], fin_sem.at[0], fin_sem.at[1], (sect, me, to)).start()
        final_ref[:, out_cols] = fin_src[...]
        wait_here(final_ref.at[:, pl.ds(0, (near_dp - 1) * part)], fin_sem.at[1])
        wait_sent(final_ref, fin_sem.at[0])
        wait_sent(final_ref.at[:, pl.ds(0, (near_dp - 1) * part)], fin_sem.at[0])

    def decode_sent(i, blocks):
        wait_sent(d1_out.at[i, pl.ds(0, experts - 1)], dec_send.at[0, i])
        wait_sent(xg_far.at[i, pl.ds(0, shards - 1)], dec_send.at[1, i])
        wait_sent(xg_near.at[i, core, pl.ds(0, nx - 1)], dec_send.at[2, i])
        wait_sent(d3_out_far.at[i, pl.ds(0, shards - 1)], dec_send.at[3, i])
        wait_sent(d3_sum.at[i, pl.ds(0, nx - 1)], dec_send.at[4, i])
        wait_sent(xg_near.at[i, core], dec_send.at[6, i])
        wait_sent(d3_out_near.at[i, core], dec_send.at[7, i])
        wait_sent(d4_out.at[i, pl.ds(0, blocks)], dec_send.at[5, i])

    @pl.when(sect == 0)
    def _():
        for i in range(2):
            tables(i, i)
        loads[0].wait()
        rows = rows_v[...].astype(f32)
        states_ref[...] = jnp.concatenate([rows[:, :LANES], rows[:, LANES:]], axis=0)
        loads[1].wait()
        loads[2].wait()
        greeted()
        rcopy(own_v, held, l1_sem.at[0], l1_sem.at[1], (other, me, dp)).start()
        loads[3].wait()
        loads[4].wait()
        decode_step(0, up_v, down_v)
        rcopy(states_ref, states_ref, st_sem.at[0], st_sem.at[1], (other, me, dp)).start()
        decode_step(1, up_v, down_v, hand_over=True)
        tables(2, 3)
        wait_sent(states_ref, st_sem.at[0])
        wait_sent(held, l1_sem.at[0])
        decode_sent(0, experts - 1)
        decode_sent(1, experts)

        @pl.when(dp < near_dp)
        def _():
            wait_here(last_ref, last_sem.at[1])
            mix(2, experts, last_ref)
            finish(last_ref)

        @pl.when(dp >= near_dp)
        def _():
            wait_here(final_ref, fin_sem.at[1])

        wait_here(fresh_up_ref, fresh_sem.at[0, 1])
        for i in range(2):
            wait_here(fresh_down_ref.at[pl.ds(i * (hidden // 2), hidden // 2)], fresh_sem.at[1 + i, 1])

    @pl.when(sect == 1)
    def _():
        lengths = len_ref[...].astype(f32)
        count = lengths.shape[1]
        length = jnp.concatenate([to_col(lengths[0:1]), to_col(lengths[1:2])], axis=0)
        both = 2 * count
        a, b = iota((both, both), 0), iota((both, both), 1)
        same_half = (a < count) == (b < count)
        start_row = jnp.sum(jnp.where(same_half & (a < b), length, 0.0), axis=0, keepdims=True)
        length_row = to_row(length)
        half_rows = held.shape[1]
        r, t = iota((2 * half_rows, both), 0), iota((2 * half_rows, both), 1)
        second = r >= half_rows
        row_in = r - jnp.where(second, float(half_rows), 0.0)
        offset = row_in - start_row
        inside = (second == (t >= count)) & (offset >= 0.0) & (offset < length_row)
        shard = pack_ref[...].astype(f32)
        target2 = jnp.sum(jnp.where(inside, shard * 8.0 + offset, 0.0), axis=1, keepdims=True)
        target2 = to_row(jnp.concatenate([target2, target2 + 4.0], axis=0))
        row_ids = iota((experts * 8, 4 * half_rows), 0)
        pack = ones_where(row_ids == target2)
        for load in loads:
            load.wait()
        for i in range(2):
            tables(i, i + 2)
        tables(2, 1)
        greeted()
        wait_here(held, l1_sem.at[1])
        for j in range(2):
            far, own = held[j], own_v[j]
            stacked = jnp.concatenate([far[:, :LANES], own[:, :LANES], far[:, LANES:], own[:, LANES:]], axis=0)
            out2[j] = dot(pack, stacked).astype(bf16).reshape(experts, 8, LANES)
            recv2[j, me] = out2[j, me]

        for k in sect_far_first:
            to = lax.rem(me + k, experts)
            rcopy(out2.at[:, to], recv2.at[:, me], l2_sem.at[0], l2_sem.at[1], (sect, to, dp)).start()

        lroutes = lroutes_ref[...].astype(f32)
        first, second = to_col(lroutes[0:1]), to_col(lroutes[1:2])
        within = ranks(first, second)
        gates = [to_col(lgates_ref[k : k + 1, :]) for k in range(2)]

        def by_half(col, step):
            n = col.shape[0]
            row = jnp.zeros((1, 2 * n), f32)
            r, l = iota((n, 2 * n), 0), iota((n, 2 * n), 1)
            source = jnp.floor(r * 0.25)
            place = source * 4.0 + r
            row += jnp.sum(jnp.where(l == place, col, 0.0), axis=0, keepdims=True)
            row += jnp.sum(jnp.where(l == place + 4.0, col + step, 0.0), axis=0, keepdims=True)
            return row

        stride = 2.0 * cap_l
        tr0 = by_half(first * stride + within[0], float(cap_l))
        tr1 = by_half(second * stride + within[1], float(cap_l))
        gr0, gr1 = by_half(gates[0], 0.0), by_half(gates[1], 0.0)
        ids = iota((experts * 2 * cap_l, experts * 8), 0)
        hit0, hit1 = ids == tr0, ids == tr1
        pick = ones_where(hit0 | hit1)
        scale = jnp.where(hit0, gr0, 0.0) + jnp.where(hit1, gr1, 0.0)
        high = scale.astype(bf16)
        low = (scale - high.astype(f32)).astype(bf16)
        wait_here(recv2.at[:, pl.ds(0, experts - 1)], l2_sem.at[1])
        inputs = recv2[0].reshape(experts * 8, LANES)
        cots = recv2[1].reshape(experts * 8, LANES)
        out3[0] = dot(pick, inputs).astype(bf16).reshape(experts, 2 * cap_l, LANES)
        out3[1] = (dot(high, cots) + dot(low, cots)).astype(bf16).reshape(experts, 2 * cap_l, LANES)
        for g in range(GROUPS):
            for k in sect_far_first:
                if k % GROUPS == g:
                    to = lax.rem(me + k, experts)
                    place = g * per + k // GROUPS
                    rcopy(out3.at[:, to], recv3.at[:, place], l3_send, l3_recv.at[g], (sect, to, dp)).start()
        recv3[0, 0] = out3[0, me]
        recv3[1, 0] = out3[1, me]

        right, left = lax.rem(ring + 1, nx), lax.rem(ring + nx - 1, nx)

        def spread(g):
            first_in = 1 if g == 0 else 0
            if per - first_in:
                wait_here(recv3.at[:, pl.ds(g * per + first_in, per - first_in)], l3_recv.at[g])
            for j in range(2):
                rows = recv3[j, g * per : (g + 1) * per].reshape(per * 2 * cap_l, LANES)
                block = [dot(take_l[c], rows).astype(bf16) for c in range(2)]
                xg4[g, core, ring, j] = jnp.concatenate(block, axis=1)
            mine = xg4.at[g, core, ring]
            rcopy(mine, mine, l4_send.at[0, g], l4_recv.at[0, g], at_ring(right)).start()
            rcopy(mine, mine, l4_send.at[1, g], l4_recv.at[1, g], at_ring(left)).start()

        def relay(g):
            from_left, from_right = xg4.at[g, core, left], xg4.at[g, core, right]
            wait_here(from_left, l4_recv.at[0, g])
            on = from_left.at[0]
            rcopy(on, on, l4_send.at[2, g], l4_recv.at[2, g], at_ring(right)).start()
            wait_here(from_right, l4_recv.at[1, g])
            on = from_right.at[1]
            rcopy(on, on, l4_send.at[3, g], l4_recv.at[3, g], at_ring(left)).start()

        def share(g):
            across = xg4.at[g, core, lax.rem(ring + 2, nx)]
            wait_here(across.at[0], l4_recv.at[2, g])
            wait_here(across.at[1], l4_recv.at[3, g])
            mine = xg4.at[g, core]
            rcopy(mine, mine, l4_send.at[4, g], l4_recv.at[4, g], (sect, me, ring * 2 + 1 - core)).start()

        def hidden_parts(g):
            wait_here(xg4.at[g, 1 - core], l4_recv.at[4, g])
            pre = jnp.zeros((group_slots, hidden), f32)
            grad = jnp.zeros((group_slots, hidden), f32)
            for q in range(shards):
                cols = slice(q * part, (q + 1) * part)
                pre += dot_nt(xg4[g, q % 2, q // 2, 0], up_v[:, cols])
                grad += dot_nt(xg4[g, q % 2, q // 2, 1], down_v[:, cols])
            pre = pre * model_scale
            grad = grad * hidden_scale
            sig = 1.0 / (1.0 + jnp.exp(-pre))
            act_ref[g] = (pre * sig).astype(bf16)
            pre_ref[g] = (grad * sig * (1.0 + pre * (1.0 - sig))).astype(bf16)

        stages = (spread, relay, share, hidden_parts)
        for n in range(GROUPS + len(stages) - 1):
            for stage, run in enumerate(stages):
                if 0 <= n - stage < GROUPS:
                    run(n - stage)

        act = jnp.concatenate([act_ref[g] for g in range(GROUPS)], axis=0)
        pre = jnp.concatenate([pre_ref[g] for g in range(GROUPS)], axis=0)
        for j, (lhs, old, new, scale) in enumerate(
            ((pre, up_v, fresh_up_ref, model_scale), (act, down_v, fresh_down_ref, hidden_scale))
        ):
            for q in range(shards):
                cols = slice(q * part, (q + 1) * part)
                rhs = jnp.concatenate([xg4[g, q % 2, q // 2, j] for g in range(GROUPS)], axis=0)
                grad = dot_tn(lhs, rhs) * scale
                new[:, cols] = (old[:, cols].astype(f32) - step_size * grad).astype(bf16)
            if j == 0:
                rcopy(new, new, fresh_sem.at[j, 0], fresh_sem.at[j, 1], (other, me, dp)).start()

        wait_here(states_ref, st_sem.at[1])
        mix(2, experts, states_ref)
        for i in range(2):

            def send_fresh(i=i):
                rows = pl.ds(i * (hidden // 2), hidden // 2)
                piece = fresh_down_ref.at[rows]
                rcopy(piece, piece, fresh_sem.at[1 + i, 0], fresh_sem.at[1 + i, 1], (other, me, dp)).start()

            decode_step(i, fresh_up_ref, fresh_down_ref, meanwhile=send_fresh, split=i == 1)
            if i == 0:

                @pl.when(dp < near_dp)
                def _():
                    rcopy(states_ref, last_ref, last_sem.at[0], last_sem.at[1], (other, me, dp)).start()

        decode_sent(0, experts - 1)

        @pl.when(dp < near_dp)
        def _():
            wait_here(final_ref, fin_sem.at[1])
            wait_sent(states_ref, last_sem.at[0])
            decode_sent(1, experts)

        @pl.when(dp >= near_dp)
        def _():
            finish(states_ref)
            decode_sent(1, experts - 1)

        wait_sent(out2.at[:, pl.ds(0, experts - 1)], l2_sem.at[0])
        wait_sent(out3.at[:, pl.ds(0, experts - 1)], l3_send)
        for g in range(GROUPS):
            wait_sent(xg4.at[g, core, ring], l4_send.at[0, g])
            wait_sent(xg4.at[g, core, ring], l4_send.at[1, g])
            wait_sent(xg4.at[g, core, ring, 0], l4_send.at[2, g])
            wait_sent(xg4.at[g, core, ring, 1], l4_send.at[3, g])
            wait_sent(xg4.at[g, core], l4_send.at[4, g])
        wait_sent(fresh_up_ref, fresh_sem.at[0, 0])
        for i in range(2):
            wait_sent(fresh_down_ref.at[pl.ds(i * (hidden // 2), hidden // 2)], fresh_sem.at[1 + i, 0])


def on_device(
    decode_states, norm_gain, decode_routes, decode_gates, up_weight, down_weight,
    traj_inputs, traj_cotangents, traj_lengths, packing, learner_routes, learner_gates,
):
    experts, shards = lax.axis_size("exp"), lax.axis_size("dp")
    dec_rows, width = decode_states.shape
    lrn_rows = learner_routes.shape[0]
    part = width // shards
    hidden = up_weight.shape[2]
    cap_d = 3 * dec_rows * 2 // (2 * experts)
    cap_l = 3 * lrn_rows * 2 // (2 * experts)
    sizes = (experts * 3 // 8, experts - experts * 3 // 8)
    pairs = (2, shards // 2)
    far, near = ((shards,), sizes[0]), (pairs, sizes[1])
    chips = (pairs[1:], sizes[1])
    buffers = (far, near, far, near, far, chips, chips, chips)
    group_slots = experts // GROUPS * cap_l
    half_rows = traj_inputs.shape[1]
    vmem = pl.BlockSpec(memory_space=pltpu.VMEM)
    hbm = pl.BlockSpec(memory_space=pltpu.HBM)
    dma = pltpu.SemaphoreType.DMA
    keep = functools.partial(pltpu.with_memory_space_constraint, memory_space=pltpu.HBM)
    final, fresh_up, fresh_down = pl.pallas_call(
        functools.partial(kernel, experts, shards, cap_d, cap_l),
        out_shape=(
            jax.ShapeDtypeStruct((dec_rows, width // 2), bf16),
            jax.ShapeDtypeStruct((hidden, width), bf16),
            jax.ShapeDtypeStruct((hidden, width), bf16),
        ),
        in_specs=[hbm, vmem, vmem, vmem, hbm, hbm, hbm, hbm, vmem, vmem, vmem, vmem],
        out_specs=(vmem,) * 3,
        scratch_shapes=[
            pltpu.VMEM((2, experts, 8, LANES), bf16),
            pltpu.VMEM((2, experts, 8, LANES), bf16),
            *[pltpu.VMEM((2, *lead, size * cap_d, part), bf16) for lead, size in buffers],
            pltpu.VMEM((2, experts, 8, LANES), bf16),
            pltpu.VMEM((3, experts, 8, LANES), bf16),
            pltpu.VMEM((2 * dec_rows, LANES), f32),
            pltpu.VMEM((2 * dec_rows, LANES), f32),
            pltpu.VMEM((3, 2, 1, 2 * dec_rows), f32),
            pltpu.VMEM((3, 2, 2 * dec_rows, 1), f32),
            pltpu.VMEM((3, 2, 2 * dec_rows, 1), f32),
            pltpu.VMEM((2, half_rows, part), bf16),
            pltpu.VMEM((2, experts, 8, LANES), bf16),
            pltpu.VMEM((2, experts, 8, LANES), bf16),
            pltpu.VMEM((2, experts, 2 * cap_l, LANES), bf16),
            pltpu.VMEM((2, experts, 2 * cap_l, LANES), bf16),
            pltpu.VMEM((GROUPS, 2, shards // 2, 2, group_slots, part), bf16),
            pltpu.VMEM((GROUPS, group_slots, hidden), bf16),
            pltpu.VMEM((GROUPS, group_slots, hidden), bf16),
            pltpu.VMEM((dec_rows, part), bf16),
            pltpu.VMEM((hidden, width), bf16),
            pltpu.VMEM((hidden, width), bf16),
            pltpu.VMEM((dec_rows, part), bf16),
            pltpu.VMEM((2, half_rows, part), bf16),
            *[pltpu.VMEM((2, size * cap_d, size * 8), bf16) for size in sizes],
            *[pltpu.VMEM((2, size * 8, size * cap_d), bf16) for size in sizes],
            pltpu.VMEM((2, group_slots, 2 * group_slots), bf16),
            dma((5,)),
            dma((8, 2)),
            dma((3,)),
            dma((3, 2, 2)),
            dma((2, 2)),
            dma((2,)),
            dma((2,)),
            dma((2,)),
            dma((2,)),
            dma((2,)),
            dma((3, 2)),
            dma,
            dma((GROUPS,)),
            dma((5, GROUPS)),
            dma((5, GROUPS)),
        ],
        compiler_params=pltpu.CompilerParams(
            collective_id=0, has_side_effects=True, vmem_limit_bytes=40 * 2**20
        ),
    )(
        keep(decode_states), keep(norm_gain.reshape(width // LANES, LANES)),
        keep(decode_routes.transpose(0, 2, 1)), keep(decode_gates.transpose(0, 2, 1)),
        keep(up_weight[0, 0]), keep(down_weight[0, 0]), keep(traj_inputs[0]), keep(traj_cotangents[0]), keep(traj_lengths[0]), keep(packing),
        keep(learner_routes.T), keep(learner_gates.T),
    )
    return final, fresh_up[None, None], fresh_down[None, None]


def solution(mesh):
    in_specs = (
        P("exp", None),
        P(),
        P(None, "exp", None),
        P(None, "exp", None),
        P("sect", "exp", "dp", None),
        P("sect", "exp", "dp", None),
        P("sect", "exp", None),
        P("sect", "exp", None),
        P("exp", None, None),
        P("exp", None),
        P("exp", None),
        P("exp", None),
    )
    out_specs = (P("exp", "sect"), P("sect", "exp", "dp", None), P("sect", "exp", "dp", None))
    return jax.shard_map(on_device, mesh=mesh, in_specs=in_specs, out_specs=out_specs, check_vma=False)
```

```python
import functools

import jax
import jax.numpy as jnp
from jax import lax
from jax.experimental import pallas as pl
from jax.experimental.pallas import tpu as pltpu
from jax.sharding import PartitionSpec as P

MESH = pl.DeviceIdType.MESH
step_size = 3.0
norm_eps = 1e-06
f32 = jnp.float32
bf16 = jnp.bfloat16
LANES = 128
GROUPS = 4


def dot(a, b):
    return lax.dot_general(a, b, (((1,), (0,)), ((), ())), preferred_element_type=f32)


def dot_nt(a, b):
    return lax.dot_general(a, b, (((1,), (1,)), ((), ())), preferred_element_type=f32)


def dot_tn(a, b):
    return lax.dot_general(a, b, (((0,), (0,)), ((), ())), preferred_element_type=f32)


def iota(shape, dim):
    return lax.broadcasted_iota(jnp.int32, shape, dim).astype(f32)


def to_row(col):
    n = col.shape[0]
    eye = iota((n, n), 0) == iota((n, n), 1)
    return jnp.sum(jnp.where(eye, col, 0.0), axis=0, keepdims=True)


def to_col(row):
    n = row.shape[1]
    eye = iota((n, n), 0) == iota((n, n), 1)
    return jnp.sum(jnp.where(eye, row, 0.0), axis=1, keepdims=True)


def ranks(first, second):
    n = first.shape[0]
    first_row, second_row = to_row(first), to_row(second)
    before = iota((n, n), 1) < iota((n, n), 0)
    out = []
    for mine in (first, second):
        same = ((first_row == mine) | (second_row == mine)) & before
        out.append(jnp.sum(jnp.where(same, 1.0, 0.0), axis=1, keepdims=True))
    return out


def far_first(count):
    return sorted(range(1, count), key=lambda k: (-min(k, count - k), k))


def slot_place(slot, per_source, block, c, half_step):
    source = jnp.floor((slot + 0.5) * (1.0 / per_source))
    return source * block + c * half_step + (slot - source * per_source)


def ones_where(condition):
    return jnp.where(condition, 1.0, 0.0).astype(bf16)


def kernel(
    experts, shards, cap_d, cap_l,
    rows_ref, gain_ref, routes_ref, gates_ref, up_ref, down_ref, in_ref, cot_ref, len_ref, pack_ref,
    lroutes_ref, lgates_ref,
    final_ref, fresh_up_ref, fresh_down_ref,
    d1_out, d1_in, xg_far, xg_near, d3_out_far, d3_out_near, d3_in_far, d3_in_near, pair_in, d3_sum, d4_out, d4_in, states_ref, last_ref, trow_ref, tcol_ref, gcol_ref,
    held, out2, recv2, out3, recv3, xg4, act_ref, pre_ref, fin_src,
    up_v, down_v, rows_v, own_v, take_far, take_near, give_far, give_near, take_l,
    load_sem, dec_send, ends_recv, half_recv, pair_recv, l1_sem, l2_sem, st_sem, last_sem, fin_sem, fresh_sem, l3_send, l3_recv, l4_send, l4_recv,
):
    sect, me, dp = lax.axis_index("sect"), lax.axis_index("exp"), lax.axis_index("dp")
    ring, core = lax.div(dp, 2), lax.rem(dp, 2)
    other = 1 - sect
    width = rows_ref.shape[1]
    part = width // shards
    hidden = up_ref.shape[0]
    model_scale = width ** (-0.5)
    hidden_scale = (hidden * shards) ** (-0.5)
    dec_rows = rows_ref.shape[0]
    per = experts // GROUPS
    group_slots = per * cap_l
    col0 = pl.multiple_of(dp * part, part)
    sizes = (experts * 3 // 8, experts - experts * 3 // 8)
    firsts = (0, sizes[0])
    low = (experts - sizes[0] + 1) // 2
    take_d, give_d = (take_far, take_near), (give_far, give_near)
    sect_far_first = far_first(experts)
    loads = [
        pltpu.make_async_copy(rows_ref.at[:, pl.ds(col0, part)], rows_v, load_sem.at[0]),
        pltpu.make_async_copy(in_ref.at[:, pl.ds(col0, part)], own_v.at[0], load_sem.at[1]),
        pltpu.make_async_copy(cot_ref.at[:, pl.ds(col0, part)], own_v.at[1], load_sem.at[2]),
        pltpu.make_async_copy(up_ref, up_v, load_sem.at[3]),
        pltpu.make_async_copy(down_ref, down_v, load_sem.at[4]),
    ]

    def rcopy(src, dst, send, recv, device):
        return pltpu.make_async_remote_copy(
            src_ref=src, dst_ref=dst, send_sem=send, recv_sem=recv, device_id=device, device_id_type=MESH
        )

    nx = shards // 2
    near_dp = shards // 2
    sibling = (sect, me, ring * 2 + 1 - core)

    def at_ring(position):
        return (sect, me, position * 2 + core)

    def wait_sent(ref, sem):
        rcopy(ref, ref, sem, sem, (sect, me, dp)).wait_send()

    def wait_here(ref, sem):
        rcopy(ref, ref, sem, sem, (sect, me, dp)).wait_recv()

    barrier = pltpu.get_barrier_semaphore()

    for k in sect_far_first:
        for home in (other, sect):
            pl.semaphore_signal(barrier, inc=1, device_id=(home, lax.rem(me + k, experts), dp), device_id_type=MESH)
    for q in range(1, shards):
        pl.semaphore_signal(barrier, inc=1, device_id=(sect, me, lax.rem(dp + q, shards)), device_id_type=MESH)
    for q in range(shards):
        pl.semaphore_signal(barrier, inc=1, device_id=(other, me, lax.rem(dp + q, shards)), device_id_type=MESH)
    for load in loads:
        load.start()
    for c in range(2):
        for h, size in enumerate(sizes):
            row, col = iota((size * cap_d, size * 8), 0), iota((size * cap_d, size * 8), 1)
            take_d[h][c] = ones_where(col == slot_place(row, cap_d, 8.0, c, 4.0))
            row, col = iota((size * 8, size * cap_d), 0), iota((size * 8, size * cap_d), 1)
            give_d[h][c] = ones_where(row == slot_place(col, cap_d, 8.0, c, 4.0))
        row, col = iota((group_slots, 2 * group_slots), 0), iota((group_slots, 2 * group_slots), 1)
        take_l[c] = ones_where(col == slot_place(row, cap_l, 2.0 * cap_l, c, float(cap_l)))

    def greeted():
        pl.semaphore_wait(barrier, 2 * (experts - 1) + shards - 1 + shards)

    def tables(i, t):
        routes = routes_ref[t].astype(f32)
        first, second = to_col(routes[0:1]), to_col(routes[1:2])
        within = ranks(first, second)
        for k, mine in enumerate((first, second)):
            target = mine * 8.0 + within[k]
            both = jnp.concatenate([target, target + 4.0], axis=0)
            tcol_ref[i, k] = both
            trow_ref[i, k] = to_row(both)
        for k in range(2):
            gate = to_col(gates_ref[t, k : k + 1, :])
            gcol_ref[i, k] = jnp.concatenate([gate, gate], axis=0)

    def prepare(i):
        gain0, gain1 = gain_ref[pl.ds(2 * dp, 1), :], gain_ref[pl.ds(2 * dp + 1, 1), :]
        gains = jnp.concatenate(
            [jnp.broadcast_to(gain0, (dec_rows, LANES)), jnp.broadcast_to(gain1, (dec_rows, LANES))], axis=0
        )
        y = (states_ref[...] * gains).astype(bf16)
        row_ids = iota((experts * 8, 2 * dec_rows), 0)
        pick = (row_ids == trow_ref[i, 0]) | (row_ids == trow_ref[i, 1])
        pick = jnp.where(pick, 1.0, 0.0).astype(bf16)
        d1_out[i] = dot(pick, y).astype(bf16).reshape(experts, 8, LANES)

    def decode_step(i, up, down, meanwhile=None, hand_over=False, split=False):
        for k in sect_far_first:
            place = (k - low) % experts
            to = lax.rem(me + k, experts)
            arrival = half_recv.at[0, i, 0 if place < sizes[0] else 1]
            rcopy(d1_out.at[i, to], d1_in.at[i, place], dec_send.at[0, i], arrival, (sect, to, dp)).start()
        own_place = experts - low
        d1_in[i, own_place] = d1_out[i, me]

        def gather(h):
            first, size = firsts[h], sizes[h]
            wait_here(d1_in.at[i, pl.ds(first, size - h)], half_recv.at[0, i, h])
            arrived = d1_in[i, first : first + size].reshape(size * 8, LANES)
            block = [dot(take_d[h][c], arrived).astype(bf16) for c in range(2)]
            if h == 0:
                xg_far[i, dp] = jnp.concatenate(block, axis=1)
                mine = xg_far.at[i, dp]
                for q in far_first(shards):
                    to = lax.rem(dp + q, shards)
                    rcopy(mine, mine, dec_send.at[1, i], half_recv.at[1, i, 0], (sect, me, to)).start()
            else:
                xg_near[i, core, ring] = jnp.concatenate(block, axis=1)
                mine = xg_near.at[i, core, ring]
                for k in far_first(nx):
                    to = at_ring(lax.rem(ring + k, nx))
                    rcopy(mine, mine, dec_send.at[2, i], half_recv.at[1, i, 1], to).start()

        def share_near():
            wait_here(xg_near.at[i, core, pl.ds(0, nx - 1)], half_recv.at[1, i, 1])
            mine = xg_near.at[i, core]
            rcopy(mine, mine, dec_send.at[6, i], pair_recv.at[0, i], sibling).start()

        def up_part(h):
            if h == 0:
                wait_here(xg_far.at[i, pl.ds(0, shards - 1)], half_recv.at[1, i, 0])
            else:
                wait_here(xg_near.at[i, 1 - core], pair_recv.at[0, i])
            before_act = jnp.zeros((sizes[h] * cap_d, hidden), f32)
            squares = jnp.zeros((sizes[h] * cap_d, part), f32)
            for q in range(shards):
                piece = xg_far[i, q] if h == 0 else xg_near[i, q % 2, q // 2]
                before_act += dot_nt(piece, up[:, q * part : (q + 1) * part])
                gain = jnp.concatenate([gain_ref[2 * q : 2 * q + 1], gain_ref[2 * q + 1 : 2 * q + 2]], axis=1)
                wide = piece.astype(f32) * (1.0 / gain)
                squares += wide * wide
            mean = jnp.sum(squares, axis=1, keepdims=True) * (1.0 / width)
            before_act = before_act * (lax.rsqrt(mean + norm_eps) * model_scale)
            return (before_act / (1.0 + jnp.exp(-before_act))).astype(bf16)

        def down_part(h, act):
            for q in range(shards):
                piece = (dot(act, down[:, q * part : (q + 1) * part]) * hidden_scale).astype(bf16)
                if h == 0:
                    d3_out_far[i, q] = piece
                else:
                    d3_out_near[i, q % 2, q // 2] = piece
            if h == 0:
                for q in far_first(shards):
                    to = lax.rem(dp + q, shards)
                    from_here, to_there = d3_out_far.at[i, to], d3_in_far.at[i, dp]
                    rcopy(from_here, to_there, dec_send.at[3, i], half_recv.at[2, i, 0], (sect, me, to)).start()
                d3_in_far[i, dp] = d3_out_far[i, dp]
            else:
                theirs = d3_out_near.at[i, 1 - core]
                rcopy(theirs, pair_in.at[i], dec_send.at[7, i], pair_recv.at[1, i], sibling).start()

        def scatter_near():
            wait_here(pair_in.at[i], pair_recv.at[1, i])
            d3_sum[i] = (d3_out_near[i, core].astype(f32) + pair_in[i].astype(f32)).astype(bf16)
            for k in far_first(nx):
                to = lax.rem(ring + k, nx)
                from_here, to_there = d3_sum.at[i, to], d3_in_near.at[i, ring]
                rcopy(from_here, to_there, dec_send.at[4, i], half_recv.at[2, i, 1], at_ring(to)).start()
            d3_in_near[i, ring] = d3_sum[i, ring]

        def give_back(h):
            first, size = firsts[h], sizes[h]
            d3_in, count = (d3_in_far, shards) if h == 0 else (d3_in_near, nx)
            wait_here(d3_in.at[i, pl.ds(0, count - 1)], half_recv.at[2, i, h])
            total = d3_in[i, 0].astype(f32)
            for q in range(1, count):
                total += d3_in[i, q].astype(f32)
            total = total.astype(bf16)
            back = dot(give_d[h][0], total[:, :LANES]) + dot(give_d[h][1], total[:, LANES:])
            d4_out[i, first : first + size] = back.astype(bf16).reshape(size, 8, LANES)
            for k in sect_far_first + ([0] if hand_over else []):
                place = (k - low) % experts
                if first <= place < first + size:
                    to = lax.rem(me + experts - k, experts)
                    home, slot = (other, 2) if hand_over else (sect, i)
                    if split:
                        home, slot = jnp.where(dp < near_dp, other, sect), jnp.where(dp < near_dp, 2, i)
                    rcopy(
                        d4_out.at[i, place], d4_in.at[slot, me], dec_send.at[5, i], ends_recv.at[slot], (home, to, dp)
                    ).start()

        gather(1)
        gather(0)
        share_near()
        if meanwhile is not None:
            meanwhile()
        near_act = up_part(1)
        down_part(0, up_part(0))
        down_part(1, near_act)
        scatter_near()
        give_back(0)
        give_back(1)
        if split:
            @pl.when(dp < near_dp)
            def _():
                rcopy(
                    d4_out.at[i, own_place], d4_in.at[2, me], dec_send.at[5, i], ends_recv.at[2], (other, me, dp)
                ).start()

            @pl.when(dp >= near_dp)
            def _():
                d4_in[i, me] = d4_out[i, own_place]
                mix(i, experts - 1, states_ref)
        elif not hand_over:
            d4_in[i, me] = d4_out[i, own_place]
            mix(i, experts - 1, states_ref)

    def mix(i, blocks, onto):
        lane_ids = iota((2 * dec_rows, experts * 8), 1)
        weight = jnp.where(lane_ids == tcol_ref[i, 0], gcol_ref[i, 0], 0.0)
        weight += jnp.where(lane_ids == tcol_ref[i, 1], gcol_ref[i, 1], 0.0)
        high = weight.astype(bf16)
        rest = weight - high.astype(f32)
        middle = rest.astype(bf16)
        lowest = (rest - middle.astype(f32)).astype(bf16)
        wait_here(d4_in.at[i, pl.ds(0, blocks)], ends_recv.at[i])
        returned = d4_in[i].reshape(experts * 8, LANES)
        onto[...] += dot(high, returned) + (dot(middle, returned) + dot(lowest, returned))

    out_cols = pl.ds(pl.multiple_of(lax.rem(dp, near_dp) * part, part), part)

    def finish(from_ref):
        last = from_ref[...].astype(bf16)
        fin_src[...] = jnp.concatenate([last[:dec_rows], last[dec_rows:]], axis=1)
        for q in far_first(shards):
            to = lax.rem(dp + q, shards)
            rcopy(fin_src, final_ref.at[:, out_cols], fin_sem.at[0], fin_sem.at[1], (sect, me, to)).start()
        final_ref[:, out_cols] = fin_src[...]
        wait_here(final_ref.at[:, pl.ds(0, (near_dp - 1) * part)], fin_sem.at[1])
        wait_sent(final_ref, fin_sem.at[0])
        wait_sent(final_ref.at[:, pl.ds(0, (near_dp - 1) * part)], fin_sem.at[0])

    def decode_sent(i, blocks):
        wait_sent(d1_out.at[i, pl.ds(0, experts - 1)], dec_send.at[0, i])
        wait_sent(xg_far.at[i, pl.ds(0, shards - 1)], dec_send.at[1, i])
        wait_sent(xg_near.at[i, core, pl.ds(0, nx - 1)], dec_send.at[2, i])
        wait_sent(d3_out_far.at[i, pl.ds(0, shards - 1)], dec_send.at[3, i])
        wait_sent(d3_sum.at[i, pl.ds(0, nx - 1)], dec_send.at[4, i])
        wait_sent(xg_near.at[i, core], dec_send.at[6, i])
        wait_sent(d3_out_near.at[i, core], dec_send.at[7, i])
        wait_sent(d4_out.at[i, pl.ds(0, blocks)], dec_send.at[5, i])

    @pl.when(sect == 0)
    def _():
        for i in range(2):
            tables(i, i)
        loads[0].wait()
        rows = rows_v[...].astype(f32)
        states_ref[...] = jnp.concatenate([rows[:, :LANES], rows[:, LANES:]], axis=0)
        prepare(0)
        for load in loads[1:]:
            load.wait()
        greeted()
        rcopy(own_v, held, l1_sem.at[0], l1_sem.at[1], (other, me, dp)).start()
        decode_step(0, up_v, down_v)
        prepare(1)
        rcopy(states_ref, states_ref, st_sem.at[0], st_sem.at[1], (other, me, dp)).start()
        decode_step(1, up_v, down_v, hand_over=True)
        tables(2, 3)
        wait_sent(states_ref, st_sem.at[0])
        wait_sent(held, l1_sem.at[0])
        decode_sent(0, experts - 1)
        decode_sent(1, experts)

        @pl.when(dp < near_dp)
        def _():
            wait_here(last_ref, last_sem.at[1])
            mix(2, experts, last_ref)
            finish(last_ref)

        @pl.when(dp >= near_dp)
        def _():
            wait_here(final_ref, fin_sem.at[1])

        wait_here(fresh_up_ref, fresh_sem.at[0, 1])
        for i in range(2):
            wait_here(fresh_down_ref.at[pl.ds(i * (hidden // 2), hidden // 2)], fresh_sem.at[1 + i, 1])

    @pl.when(sect == 1)
    def _():
        lengths = len_ref[...].astype(f32)
        count = lengths.shape[1]
        length = jnp.concatenate([to_col(lengths[0:1]), to_col(lengths[1:2])], axis=0)
        both = 2 * count
        a, b = iota((both, both), 0), iota((both, both), 1)
        same_half = (a < count) == (b < count)
        start_row = jnp.sum(jnp.where(same_half & (a < b), length, 0.0), axis=0, keepdims=True)
        length_row = to_row(length)
        half_rows = held.shape[1]
        r, t = iota((2 * half_rows, both), 0), iota((2 * half_rows, both), 1)
        second = r >= half_rows
        row_in = r - jnp.where(second, float(half_rows), 0.0)
        offset = row_in - start_row
        inside = (second == (t >= count)) & (offset >= 0.0) & (offset < length_row)
        shard = pack_ref[...].astype(f32)
        target2 = jnp.sum(jnp.where(inside, shard * 8.0 + offset, 0.0), axis=1, keepdims=True)
        target2 = to_row(jnp.concatenate([target2, target2 + 4.0], axis=0))
        row_ids = iota((experts * 8, 4 * half_rows), 0)
        pack = ones_where(row_ids == target2)
        for load in loads:
            load.wait()
        for i in range(2):
            tables(i, i + 2)
        tables(2, 1)
        greeted()
        wait_here(held, l1_sem.at[1])
        for j in range(2):
            far, own = held[j], own_v[j]
            stacked = jnp.concatenate([far[:, :LANES], own[:, :LANES], far[:, LANES:], own[:, LANES:]], axis=0)
            out2[j] = dot(pack, stacked).astype(bf16).reshape(experts, 8, LANES)
            recv2[j, me] = out2[j, me]

        for k in sect_far_first:
            to = lax.rem(me + k, experts)
            rcopy(out2.at[:, to], recv2.at[:, me], l2_sem.at[0], l2_sem.at[1], (sect, to, dp)).start()

        lroutes = lroutes_ref[...].astype(f32)
        first, second = to_col(lroutes[0:1]), to_col(lroutes[1:2])
        within = ranks(first, second)
        gates = [to_col(lgates_ref[k : k + 1, :]) for k in range(2)]

        def by_half(col, step):
            n = col.shape[0]
            row = jnp.zeros((1, 2 * n), f32)
            r, l = iota((n, 2 * n), 0), iota((n, 2 * n), 1)
            source = jnp.floor(r * 0.25)
            place = source * 4.0 + r
            row += jnp.sum(jnp.where(l == place, col, 0.0), axis=0, keepdims=True)
            row += jnp.sum(jnp.where(l == place + 4.0, col + step, 0.0), axis=0, keepdims=True)
            return row

        stride = 2.0 * cap_l
        tr0 = by_half(first * stride + within[0], float(cap_l))
        tr1 = by_half(second * stride + within[1], float(cap_l))
        gr0, gr1 = by_half(gates[0], 0.0), by_half(gates[1], 0.0)
        ids = iota((experts * 2 * cap_l, experts * 8), 0)
        hit0, hit1 = ids == tr0, ids == tr1
        pick = ones_where(hit0 | hit1)
        scale = jnp.where(hit0, gr0, 0.0) + jnp.where(hit1, gr1, 0.0)
        high = scale.astype(bf16)
        low = (scale - high.astype(f32)).astype(bf16)
        wait_here(recv2.at[:, pl.ds(0, experts - 1)], l2_sem.at[1])
        inputs = recv2[0].reshape(experts * 8, LANES)
        cots = recv2[1].reshape(experts * 8, LANES)
        out3[0] = dot(pick, inputs).astype(bf16).reshape(experts, 2 * cap_l, LANES)
        out3[1] = (dot(high, cots) + dot(low, cots)).astype(bf16).reshape(experts, 2 * cap_l, LANES)
        for g in range(GROUPS):
            for k in sect_far_first:
                if k % GROUPS == g:
                    to = lax.rem(me + k, experts)
                    place = g * per + k // GROUPS
                    rcopy(out3.at[:, to], recv3.at[:, place], l3_send, l3_recv.at[g], (sect, to, dp)).start()
        recv3[0, 0] = out3[0, me]
        recv3[1, 0] = out3[1, me]

        right, left = lax.rem(ring + 1, nx), lax.rem(ring + nx - 1, nx)

        def spread(g):
            first_in = 1 if g == 0 else 0
            if per - first_in:
                wait_here(recv3.at[:, pl.ds(g * per + first_in, per - first_in)], l3_recv.at[g])
            for j in range(2):
                rows = recv3[j, g * per : (g + 1) * per].reshape(per * 2 * cap_l, LANES)
                block = [dot(take_l[c], rows).astype(bf16) for c in range(2)]
                xg4[g, core, ring, j] = jnp.concatenate(block, axis=1)
            mine = xg4.at[g, core, ring]
            rcopy(mine, mine, l4_send.at[0, g], l4_recv.at[0, g], at_ring(right)).start()
            rcopy(mine, mine, l4_send.at[1, g], l4_recv.at[1, g], at_ring(left)).start()

        def relay(g):
            from_left, from_right = xg4.at[g, core, left], xg4.at[g, core, right]
            wait_here(from_left, l4_recv.at[0, g])
            on = from_left.at[0]
            rcopy(on, on, l4_send.at[2, g], l4_recv.at[2, g], at_ring(right)).start()
            wait_here(from_right, l4_recv.at[1, g])
            on = from_right.at[1]
            rcopy(on, on, l4_send.at[3, g], l4_recv.at[3, g], at_ring(left)).start()

        def share(g):
            across = xg4.at[g, core, lax.rem(ring + 2, nx)]
            wait_here(across.at[0], l4_recv.at[2, g])
            wait_here(across.at[1], l4_recv.at[3, g])
            mine = xg4.at[g, core]
            rcopy(mine, mine, l4_send.at[4, g], l4_recv.at[4, g], (sect, me, ring * 2 + 1 - core)).start()

        def hidden_parts(g):
            wait_here(xg4.at[g, 1 - core], l4_recv.at[4, g])
            pre = jnp.zeros((group_slots, hidden), f32)
            grad = jnp.zeros((group_slots, hidden), f32)
            for q in range(shards):
                cols = slice(q * part, (q + 1) * part)
                pre += dot_nt(xg4[g, q % 2, q // 2, 0], up_v[:, cols])
                grad += dot_nt(xg4[g, q % 2, q // 2, 1], down_v[:, cols])
            pre = pre * model_scale
            grad = grad * hidden_scale
            sig = 1.0 / (1.0 + jnp.exp(-pre))
            act_ref[g] = (pre * sig).astype(bf16)
            pre_ref[g] = (grad * sig * (1.0 + pre * (1.0 - sig))).astype(bf16)

        stages = (spread, relay, share, hidden_parts)
        for n in range(GROUPS + len(stages) - 1):
            for stage, run in enumerate(stages):
                if 0 <= n - stage < GROUPS:
                    run(n - stage)

        act = jnp.concatenate([act_ref[g] for g in range(GROUPS)], axis=0)
        pre = jnp.concatenate([pre_ref[g] for g in range(GROUPS)], axis=0)
        for j, (lhs, old, new, scale) in enumerate(
            ((pre, up_v, fresh_up_ref, model_scale), (act, down_v, fresh_down_ref, hidden_scale))
        ):
            for q in range(shards):
                cols = slice(q * part, (q + 1) * part)
                rhs = jnp.concatenate([xg4[g, q % 2, q // 2, j] for g in range(GROUPS)], axis=0)
                grad = dot_tn(lhs, rhs) * scale
                new[:, cols] = (old[:, cols].astype(f32) - step_size * grad).astype(bf16)
            if j == 0:
                rcopy(new, new, fresh_sem.at[j, 0], fresh_sem.at[j, 1], (other, me, dp)).start()

        wait_here(states_ref, st_sem.at[1])
        mix(2, experts, states_ref)
        for i in range(2):

            def send_fresh(i=i):
                rows = pl.ds(i * (hidden // 2), hidden // 2)
                piece = fresh_down_ref.at[rows]
                rcopy(piece, piece, fresh_sem.at[1 + i, 0], fresh_sem.at[1 + i, 1], (other, me, dp)).start()

            prepare(i)
            decode_step(i, fresh_up_ref, fresh_down_ref, meanwhile=send_fresh, split=i == 1)
            if i == 0:

                @pl.when(dp < near_dp)
                def _():
                    rcopy(states_ref, last_ref, last_sem.at[0], last_sem.at[1], (other, me, dp)).start()

        decode_sent(0, experts - 1)

        @pl.when(dp < near_dp)
        def _():
            wait_here(final_ref, fin_sem.at[1])
            wait_sent(states_ref, last_sem.at[0])
            decode_sent(1, experts)

        @pl.when(dp >= near_dp)
        def _():
            finish(states_ref)
            decode_sent(1, experts - 1)

        wait_sent(out2.at[:, pl.ds(0, experts - 1)], l2_sem.at[0])
        wait_sent(out3.at[:, pl.ds(0, experts - 1)], l3_send)
        for g in range(GROUPS):
            wait_sent(xg4.at[g, core, ring], l4_send.at[0, g])
            wait_sent(xg4.at[g, core, ring], l4_send.at[1, g])
            wait_sent(xg4.at[g, core, ring, 0], l4_send.at[2, g])
            wait_sent(xg4.at[g, core, ring, 1], l4_send.at[3, g])
            wait_sent(xg4.at[g, core], l4_send.at[4, g])
        wait_sent(fresh_up_ref, fresh_sem.at[0, 0])
        for i in range(2):
            wait_sent(fresh_down_ref.at[pl.ds(i * (hidden // 2), hidden // 2)], fresh_sem.at[1 + i, 0])


def on_device(
    decode_states, norm_gain, decode_routes, decode_gates, up_weight, down_weight,
    traj_inputs, traj_cotangents, traj_lengths, packing, learner_routes, learner_gates,
):
    experts, shards = lax.axis_size("exp"), lax.axis_size("dp")
    dec_rows, width = decode_states.shape
    lrn_rows = learner_routes.shape[0]
    part = width // shards
    hidden = up_weight.shape[2]
    cap_d = 3 * dec_rows * 2 // (2 * experts)
    cap_l = 3 * lrn_rows * 2 // (2 * experts)
    sizes = (experts * 3 // 8, experts - experts * 3 // 8)
    pairs = (2, shards // 2)
    far, near = ((shards,), sizes[0]), (pairs, sizes[1])
    chips = (pairs[1:], sizes[1])
    buffers = (far, near, far, near, far, chips, chips, chips)
    group_slots = experts // GROUPS * cap_l
    half_rows = traj_inputs.shape[1]
    vmem = pl.BlockSpec(memory_space=pltpu.VMEM)
    hbm = pl.BlockSpec(memory_space=pltpu.HBM)
    dma = pltpu.SemaphoreType.DMA
    keep = functools.partial(pltpu.with_memory_space_constraint, memory_space=pltpu.HBM)
    final, fresh_up, fresh_down = pl.pallas_call(
        functools.partial(kernel, experts, shards, cap_d, cap_l),
        out_shape=(
            jax.ShapeDtypeStruct((dec_rows, width // 2), bf16),
            jax.ShapeDtypeStruct((hidden, width), bf16),
            jax.ShapeDtypeStruct((hidden, width), bf16),
        ),
        in_specs=[hbm, vmem, vmem, vmem, hbm, hbm, hbm, hbm, vmem, vmem, vmem, vmem],
        out_specs=(vmem,) * 3,
        scratch_shapes=[
            pltpu.VMEM((2, experts, 8, LANES), bf16),
            pltpu.VMEM((2, experts, 8, LANES), bf16),
            *[pltpu.VMEM((2, *lead, size * cap_d, part), bf16) for lead, size in buffers],
            pltpu.VMEM((2, experts, 8, LANES), bf16),
            pltpu.VMEM((3, experts, 8, LANES), bf16),
            pltpu.VMEM((2 * dec_rows, LANES), f32),
            pltpu.VMEM((2 * dec_rows, LANES), f32),
            pltpu.VMEM((3, 2, 1, 2 * dec_rows), f32),
            pltpu.VMEM((3, 2, 2 * dec_rows, 1), f32),
            pltpu.VMEM((3, 2, 2 * dec_rows, 1), f32),
            pltpu.VMEM((2, half_rows, part), bf16),
            pltpu.VMEM((2, experts, 8, LANES), bf16),
            pltpu.VMEM((2, experts, 8, LANES), bf16),
            pltpu.VMEM((2, experts, 2 * cap_l, LANES), bf16),
            pltpu.VMEM((2, experts, 2 * cap_l, LANES), bf16),
            pltpu.VMEM((GROUPS, 2, shards // 2, 2, group_slots, part), bf16),
            pltpu.VMEM((GROUPS, group_slots, hidden), bf16),
            pltpu.VMEM((GROUPS, group_slots, hidden), bf16),
            pltpu.VMEM((dec_rows, part), bf16),
            pltpu.VMEM((hidden, width), bf16),
            pltpu.VMEM((hidden, width), bf16),
            pltpu.VMEM((dec_rows, part), bf16),
            pltpu.VMEM((2, half_rows, part), bf16),
            *[pltpu.VMEM((2, size * cap_d, size * 8), bf16) for size in sizes],
            *[pltpu.VMEM((2, size * 8, size * cap_d), bf16) for size in sizes],
            pltpu.VMEM((2, group_slots, 2 * group_slots), bf16),
            dma((5,)),
            dma((8, 2)),
            dma((3,)),
            dma((3, 2, 2)),
            dma((2, 2)),
            dma((2,)),
            dma((2,)),
            dma((2,)),
            dma((2,)),
            dma((2,)),
            dma((3, 2)),
            dma,
            dma((GROUPS,)),
            dma((5, GROUPS)),
            dma((5, GROUPS)),
        ],
        compiler_params=pltpu.CompilerParams(
            collective_id=0, has_side_effects=True, vmem_limit_bytes=40 * 2**20
        ),
    )(
        keep(decode_states), keep(norm_gain.reshape(width // LANES, LANES)),
        keep(decode_routes.transpose(0, 2, 1)), keep(decode_gates.transpose(0, 2, 1)),
        keep(up_weight[0, 0]), keep(down_weight[0, 0]), keep(traj_inputs[0]), keep(traj_cotangents[0]), keep(traj_lengths[0]), keep(packing),
        keep(learner_routes.T), keep(learner_gates.T),
    )
    return final, fresh_up[None, None], fresh_down[None, None]


def solution(mesh):
    in_specs = (
        P("exp", None),
        P(),
        P(None, "exp", None),
        P(None, "exp", None),
        P("sect", "exp", "dp", None),
        P("sect", "exp", "dp", None),
        P("sect", "exp", None),
        P("sect", "exp", None),
        P("exp", None, None),
        P("exp", None),
        P("exp", None),
        P("exp", None),
    )
    out_specs = (P("exp", "sect"), P("sect", "exp", "dp", None), P("sect", "exp", "dp", None))
    return jax.shard_map(on_device, mesh=mesh, in_specs=in_specs, out_specs=out_specs, check_vma=False)
```
